128 devices in a mesh: segment: 2 (over z_hi), ctx: 16 (over z_lo, y, core), mp: 4 (over x).
Axes of the slice: x: 4, y: 4, z: 4 (z_hi: 2, z_lo: 2; z = z_hi * 2 + z_lo), core: 2. Of those that a mesh axis runs over, the one named last changes fastest.
Arguments:
- targets: bfloat16 [8192, 4096], P('ctx'), may hold values from -6 to 6
- memory: bfloat16 [4096, 4096], P('ctx'), may hold values from -6 to 6
- pad_counts: int32 [16], P('ctx'), may hold values from 0 to 256, as said below
- norm_gains: float32 [2, 4096], P('segment'), may hold values from 0.5 to 4
- proj_weights: bfloat16 [2, 4096, 2, 4096], P('segment', None, None, 'mp'), may hold values from -0.09375 to 0.09375
Outputs:
- scored: bfloat16 [8192, 4096], P('ctx', ('segment', 'mp'))
The draws below stay inside these ranges and needn't reach their ends.
Inputs may be any that keep to these rules, and one draw needn't show every extreme that they name: `pad_counts`: the live memory rows form one prefix: blocks before the one holding its end are full, later blocks are all padding. The first block is full and the last block is all padding in every draw.
All inputs are finite; a program needn't handle non-finite values.
Results may differ from the reference program's by a relative error of at most 0.02.
The reference program's roundings to bfloat16 on the way count: a program that leaves them out, or rounds other values in their place, can miss the bound.
Values may be sent and summed in bfloat16 or wider, within the bound.
No kernel may reach another device: no remote copies, remote signals or barrier semaphores. Data moves between devices by JAX's collectives and lax.ppermute only.
A program may use at most 256 MiB of HBM per device.

```python
import jax
import jax.numpy as jnp
from jax import lax

D = 4096
HEADS = 16
HEAD_DIM = 256
MEM_DEV = 256
TGT_TOK = 8192
MEM_TOK = 4096
N_SEGMENT = 2
N_CTX = 16


def draw_pad_counts(key, part):
    key = jax.random.fold_in(key, 11)
    live_length = jax.random.randint(key, (), MEM_DEV, MEM_TOK - MEM_DEV + 1)
    block_starts = jnp.arange(N_CTX, dtype=jnp.int32) * MEM_DEV
    live_rows = jnp.clip(live_length - block_starts, 0, MEM_DEV)
    return (MEM_DEV - live_rows).astype(jnp.int32)


def draw_norm_gains(key, part):
    key = jax.random.fold_in(key, 12)
    gain_rows = jax.random.uniform(key, (N_SEGMENT, D), jnp.float32, 0.5, 1.5)
    return gain_rows


def block_levels(stream_key, shape, pieces, least, largest):
    loudness, own = 1.0, jax.random.fold_in(stream_key, 6)
    for dim, blocks in pieces:
        heights = jnp.exp(jax.random.uniform(jax.random.fold_in(own, dim), (blocks,), jnp.float32, least / len(pieces), largest / len(pieces)))
        loudness = loudness * jnp.repeat(heights, shape[dim] // blocks).reshape([-1 if axis == dim else 1 for axis in range(len(shape))])
    return loudness


def centred(key, shape, width, most, split=(), kind=jnp.bfloat16):
    drawn = width * jax.random.normal(key, shape, jnp.float32)
    if split:
        drawn = drawn * block_levels(key, shape, split, -0.22, 0.18)
    return jnp.clip(drawn, -most, most).astype(kind)


def setup_inputs(seed: int = 0) -> dict:
    streams_of = jax.random.split(jax.random.key(seed), 6)
    return {
        "targets": centred(streams_of[0], (TGT_TOK, D), 1.0, 6.0, ((0, 16),)),
        "memory": centred(streams_of[1], (MEM_TOK, D), 1.0, 6.0, ((0, 16),)),
        "pad_counts": draw_pad_counts(jax.random.fold_in(streams_of[5], 71), 0),
        "norm_gains": draw_norm_gains(jax.random.fold_in(streams_of[5], 71), 0),
        "proj_weights": centred(streams_of[4], (N_SEGMENT, D, 2, HEADS * HEAD_DIM), D ** -0.5, 0.09375, ((0, 2), (3, 4))),
    }


def norm_rows(hidden_rows, gain_row):
    widened = hidden_rows.astype(jnp.float32)
    inverse = lax.rsqrt(lax.optimization_barrier(jnp.mean(widened * widened, axis=-1, keepdims=True)) + 1e-06)
    return (widened * inverse * gain_row).astype(jnp.bfloat16)

def reference(targets, memory, pad_counts, norm_gains, proj_weights):
    enc_normed = norm_rows(memory, norm_gains[0])
    dec_normed = norm_rows(targets, norm_gains[1])
    keys = jnp.dot(enc_normed, proj_weights[0, :, 0, :], preferred_element_type=jnp.float32).astype(jnp.bfloat16)
    values = jnp.dot(enc_normed, proj_weights[0, :, 1, :], preferred_element_type=jnp.float32).astype(jnp.bfloat16)
    queries = jnp.dot(dec_normed, proj_weights[1, :, 0, :], preferred_element_type=jnp.float32).astype(jnp.bfloat16)
    position = jnp.arange(MEM_TOK, dtype=jnp.int32)
    live_keys = position % MEM_DEV < MEM_DEV - pad_counts[position // MEM_DEV]

    def per_head(operands):
        query_head, key_head, value_head = operands
        scores = jnp.dot(query_head, key_head.T, preferred_element_type=jnp.float32)
        scores = jnp.where(live_keys[None, :], scores, -jnp.inf)
        row_peaks = lax.optimization_barrier(jnp.max(scores, axis=1, keepdims=True))
        soft_weights = jnp.where(live_keys[None, :], jnp.exp(scores - row_peaks), 0.0)
        totals = lax.optimization_barrier(jnp.sum(soft_weights, axis=1, keepdims=True))
        weighted = jnp.dot(soft_weights.astype(jnp.bfloat16), value_head, preferred_element_type=jnp.float32)
        return weighted / totals
    query_heads = queries.reshape(TGT_TOK, HEADS, HEAD_DIM).transpose(1, 0, 2)
    key_heads = keys.reshape(MEM_TOK, HEADS, HEAD_DIM).transpose(1, 0, 2)
    value_heads = values.reshape(MEM_TOK, HEADS, HEAD_DIM).transpose(1, 0, 2)
    context = lax.map(per_head, (query_heads, key_heads, value_heads))
    context = context.transpose(1, 0, 2).reshape(TGT_TOK, HEADS * HEAD_DIM).astype(jnp.bfloat16)
    mixed = jnp.dot(context, proj_weights[1, :, 1, :].T, preferred_element_type=jnp.float32)
    return (targets.astype(jnp.float32) + mixed).astype(jnp.bfloat16)
```

```python
import functools

import jax
import jax.numpy as jnp
from jax import lax
from jax.experimental import pallas as pl
from jax.experimental.pallas import tpu as pltpu
from jax.sharding import PartitionSpec as P

HEADS = 16
AXES = ("segment", "ctx", "mp")
MARK_ROWS = 16
DEAD = -1e30
VMEM = 56 * 2**20


def device_of(x, y, z, core):
    return (z // 2) * 64 + (z % 2) * 32 + y * 8 + core * 4 + x


def place_of(i):
    return i % 4, (i // 8) % 4, (i // 64) * 2 + (i // 32) % 2, (i // 4) % 2


def moved(block, step, senders=lambda x, y, z, core: True):
    route = []
    for i in range(128):
        place = place_of(i)
        if senders(*place):
            x, y, z, core = step(*place)
            route.append((i, device_of(x % 4, y % 4, z % 4, core % 2)))
    return lax.ppermute(block, AXES, route)


def along_x(block, d):
    return moved(block, lambda x, y, z, c: (x + d, y, z, c))


def along_y(block, d, senders=lambda x, y, z, core: True):
    return moved(block, lambda x, y, z, c: (x, y + d, z, c), senders)


def along_z(block, d):
    return moved(block, lambda x, y, z, c: (x, y, z + d, c))


def other_core(block, senders=lambda x, y, z, core: True):
    return moved(block, lambda x, y, z, c: (x, y, z, c + 1), senders)


def norm_rows(hidden_rows, gain_row):
    widened = hidden_rows.astype(jnp.float32)
    inverse = lax.rsqrt(jnp.mean(widened * widened, axis=-1, keepdims=True) + 1e-06)
    return (widened * inverse * gain_row).astype(jnp.bfloat16)


def normed_into(x_ref, gain_ref, normed, depth):
    rows = x_ref.shape[0]
    for top in range(0, rows, 128):
        part = norm_rows(x_ref[pl.ds(top, 128), :], gain_ref[...])
        for j in range(normed.shape[0]):
            normed[j, pl.ds(top, 128), :] = part[:, j * depth : (j + 1) * depth]


def encode_kernel(pad_ref, x_ref, gain_ref, w_ref, out_ref, normed, total):
    k, steps = pl.program_id(0), pl.num_programs(0)
    depth, width = w_ref.shape[1], w_ref.shape[3]
    rows = x_ref.shape[0]
    dim = out_ref.shape[2]

    @pl.when(k == 0)
    def _():
        normed_into(x_ref, gain_ref, normed, depth)
        total[...] = jnp.zeros_like(total)

    both = w_ref[0].reshape(depth, 2 * width)
    total[...] += jnp.dot(normed[k], both, preferred_element_type=jnp.float32)

    @pl.when(k == steps - 1)
    def _():
        position = lax.broadcasted_iota(jnp.int32, (MARK_ROWS, dim), 1)
        marks = jnp.where(position < rows - pad_ref[0], 0.0, DEAD).astype(jnp.bfloat16)
        for h in range(out_ref.shape[0]):
            out_ref[h, :rows, :] = total[:, h * dim : (h + 1) * dim].astype(jnp.bfloat16)
            out_ref[h, rows : 2 * rows, :] = total[
                :, width + h * dim : width + (h + 1) * dim
            ].astype(jnp.bfloat16)
            out_ref[h, 2 * rows :, :] = marks


def encode(memory, pad_counts, gains, weights, heads, dim):
    rows, model = memory.shape
    depth, width = 512, weights.shape[3]
    return pl.pallas_call(
        encode_kernel,
        grid=(model // depth,),
        in_specs=[
            pl.BlockSpec(memory_space=pltpu.SMEM),
            pl.BlockSpec((rows, model), lambda k: (0, 0)),
            pl.BlockSpec((1, model), lambda k: (0, 0)),
            pl.BlockSpec((1, depth, 2, width), lambda k: (0, k, 0, 0)),
        ],
        out_specs=pl.BlockSpec((heads, 2 * rows + MARK_ROWS, dim), lambda k: (0, 0, 0)),
        out_shape=jax.ShapeDtypeStruct((heads, 2 * rows + MARK_ROWS, dim), jnp.bfloat16),
        scratch_shapes=[
            pltpu.VMEM((model // depth, rows, depth), jnp.bfloat16),
            pltpu.VMEM((rows, 2 * width), jnp.float32),
        ],
        compiler_params=pltpu.CompilerParams(vmem_limit_bytes=VMEM),
    )(pad_counts, memory, gains, weights)


def query_kernel(x_ref, gain_ref, w_ref, out_ref, own_ref, normed, total):
    k, steps = pl.program_id(0), pl.num_programs(0)
    depth, width = w_ref.shape[1], w_ref.shape[3]
    rows = x_ref.shape[0]
    dim = out_ref.shape[2]

    @pl.when(k == 0)
    def _():
        normed_into(x_ref, gain_ref, normed, depth)
        total[...] = jnp.zeros_like(total)

    both = w_ref[0].reshape(depth, 2 * width)
    total[...] += jnp.dot(normed[k], both[:, :width], preferred_element_type=jnp.float32)

    @pl.when(k >= steps // 2)
    def _():
        own_ref[...] = both[:, width:]

    @pl.when(k == steps - 1)
    def _():
        for h in range(out_ref.shape[0]):
            out_ref[h, :rows, :] = total[:, h * dim : (h + 1) * dim].astype(jnp.bfloat16)
            out_ref[h, rows:, :] = jnp.zeros((MARK_ROWS, dim), jnp.bfloat16)


def query(targets, gains, weights, heads, dim):
    rows, model = targets.shape
    depth, width = 512, weights.shape[3]
    steps = model // depth
    return pl.pallas_call(
        query_kernel,
        grid=(steps,),
        in_specs=[
            pl.BlockSpec((rows, model), lambda k: (0, 0)),
            pl.BlockSpec((1, model), lambda k: (0, 0)),
            pl.BlockSpec((1, depth, 2, width), lambda k: (0, k, 0, 0)),
        ],
        out_specs=[
            pl.BlockSpec((heads, rows + MARK_ROWS, dim), lambda k: (0, 0, 0)),
            pl.BlockSpec((depth, width), lambda k: (jnp.maximum(k - steps // 2, 0), 0)),
        ],
        out_shape=[
            jax.ShapeDtypeStruct((heads, rows + MARK_ROWS, dim), jnp.bfloat16),
            jax.ShapeDtypeStruct((model // 2, width), jnp.bfloat16),
        ],
        scratch_shapes=[
            pltpu.VMEM((steps, rows, depth), jnp.bfloat16),
            pltpu.VMEM((rows, width), jnp.float32),
        ],
        compiler_params=pltpu.CompilerParams(vmem_limit_bytes=VMEM),
    )(targets, gains, weights)


def attend_kernel(place_ref, q_ref, *refs):
    blocks, out_ref, scores = refs[:-2], refs[-2], refs[-1]
    queries = q_ref[0]
    rows, keys = queries.shape[0], (blocks[0].shape[1] - MARK_ROWS) // 2
    pieces = [(ref, j) for ref in blocks for j in range(ref.shape[0])]
    peak = jnp.full((rows, keys), DEAD, jnp.float32)
    for i, (ref, j) in enumerate(pieces):
        marks = ref[j, 2 * keys : 2 * keys + 1, :].astype(jnp.float32)
        found = lax.dot_general(
            queries, ref[j, :keys, :], (((1,), (1,)), ((), ())), preferred_element_type=jnp.float32
        )
        found = found + marks
        scores[:, i * keys : (i + 1) * keys] = found
        peak = jnp.maximum(peak, found)
    peak = jnp.max(peak, axis=1, keepdims=True)
    total = jnp.zeros((rows, keys), jnp.float32)
    mixed = jnp.zeros((rows, out_ref.shape[2]), jnp.float32)
    for i, (ref, j) in enumerate(pieces):
        soft = jnp.exp(scores[:, i * keys : (i + 1) * keys] - peak)
        total = total + soft
        mixed = mixed + jnp.dot(
            soft.astype(jnp.bfloat16), ref[j, keys : 2 * keys, :], preferred_element_type=jnp.float32
        )
    out_ref[0] = (mixed / jnp.sum(total, axis=1, keepdims=True)).astype(jnp.bfloat16)


def attend(slabs, z, blocks):
    dim = slabs.shape[2]
    rows = slabs.shape[1] - MARK_ROWS
    keys = sum(b.shape[0] for b in blocks) * (blocks[0].shape[1] - MARK_ROWS) // 2
    return pl.pallas_call(
        attend_kernel,
        grid_spec=pltpu.PrefetchScalarGridSpec(
            num_scalar_prefetch=1,
            grid=(2,),
            in_specs=[
                pl.BlockSpec((1, rows, dim), lambda i, place: ((place[0] + 2 - i) % 4, 0, 0))
            ]
            + [pl.BlockSpec(b.shape, lambda i, place: (0, 0, 0)) for b in blocks],
            out_specs=pl.BlockSpec((1, rows, dim), lambda i, place: (i, 0, 0)),
            scratch_shapes=[pltpu.VMEM((rows, keys), jnp.float32)],
        ),
        out_shape=jax.ShapeDtypeStruct((2, rows, dim), jnp.bfloat16),
        compiler_params=pltpu.CompilerParams(vmem_limit_bytes=VMEM),
    )(z.reshape(1), slabs, *blocks)


def project_kernel(place_ref, c0, c1, c2, c3, w_ref, *rest):
    out_refs, context = rest[:-1], rest[-1]
    step = pl.program_id(0)
    dim = c0.shape[1]

    @pl.when(step == 0)
    def _():
        for d, ref in enumerate((c0, c1, c2, c3)):
            head = (place_ref[0] + 4 - d) % 4
            context[:, pl.ds(pl.multiple_of(head * dim, dim), dim)] = ref[...]

    mixed = lax.dot_general(
        context[...], w_ref[...], (((1,), (1,)), ((), ())), preferred_element_type=jnp.float32
    )
    for d, ref in enumerate(out_refs):

        @pl.when(step == d)
        def _(ref=ref):
            ref[...] = mixed.astype(ref.dtype)


def project(contexts, own, place, first, count, dtype):
    rows, dim = contexts[0].shape
    width = own.shape[0] // 4
    whole = pl.BlockSpec((rows, dim), lambda i, place: (0, 0))
    return pl.pallas_call(
        project_kernel,
        grid_spec=pltpu.PrefetchScalarGridSpec(
            num_scalar_prefetch=1,
            grid=(count,),
            in_specs=[whole] * 4
            + [pl.BlockSpec((width, own.shape[1]), lambda i, place: ((place[1] + first + i) % 4, 0))],
            out_specs=[pl.BlockSpec((rows, width), lambda i, place: (0, 0))] * count,
            scratch_shapes=[pltpu.VMEM((rows, 4 * dim), jnp.bfloat16)],
        ),
        out_shape=[jax.ShapeDtypeStruct((rows, width), dtype)] * count,
        compiler_params=pltpu.CompilerParams(vmem_limit_bytes=VMEM),
    )(place, *contexts, own)


def pick(stacked, index):
    return lax.dynamic_index_in_dim(stacked, index % stacked.shape[0], 0, keepdims=False)


def local(targets, memory, pad_counts, norm_gains, proj_weights):
    segment, ctx, x = (lax.axis_index(axis) for axis in AXES)
    core, y, low = ctx % 2, (ctx // 2) % 4, ctx // 8
    z = 2 * segment + low
    model, width = proj_weights.shape[1], proj_weights.shape[3]
    heads = HEADS // 4
    dim = width // heads
    rows = targets.shape[0]
    half = model // 2

    piece = half // 16
    share = lax.dynamic_slice_in_dim(proj_weights[0], ((1 - low) * 8 + ctx % 8) * piece, piece, 0)
    share = share[:, 1, :]
    down = lambda x, y, z, c: (x, y, 3 - z, c)
    share = moved(share, down, lambda x, y, z, c: z >= 2)
    encoder = lambda x, y, z, c: z < 2
    swapped = moved(share, lambda x, y, z, c: (x, y, 1 - z, c), encoder)
    first = low == 0
    share = jnp.stack([jnp.where(first, share, swapped), jnp.where(first, swapped, share)])
    gathered = jnp.zeros((2, 4, 2, piece, width), jnp.bfloat16)
    for d in (0, 1, 3, 2):
        got = share if d == 0 else along_y(share, d, encoder)
        twin = other_core(got, encoder)
        for c, part in ((core, got), (1 - core, twin)):
            gathered = lax.dynamic_update_slice(
                gathered, part[:, None, None], (0, (y - d) % 4, c, 0, 0)
            )

    slabs, own = lax.cond(
        segment == 0,
        lambda: (
            encode(memory, pad_counts, norm_gains, proj_weights, heads, dim),
            jnp.zeros((half, width), jnp.bfloat16),
        ),
        lambda: tuple(query(targets, norm_gains, proj_weights, heads, dim)),
    )
    arrived = {0: pick(slabs, z)}
    for d in (2, 1, 3):
        arrived[d] = along_z(pick(slabs, z + d), d)
    arrived = jnp.stack([arrived[d] for d in range(4)])
    block = jnp.stack([pick(arrived, z), pick(arrived, z - 1)])
    blocks = [block] + [along_y(block, d) for d in (2, 1, 3)]
    blocks = blocks + [other_core(b) for b in blocks]
    context = attend(arrived, z, blocks)

    contexts = {0: pick(context, low)}
    for d in (2, 1, 3):
        contexts[d] = along_z(pick(context, low + d), d)
    contexts = [contexts[d] for d in range(4)]
    place = jnp.stack([z, x])
    own = jnp.where(segment == 1, own, gathered.reshape(half, width))
    far = project(contexts, own, place, 1, 3, jnp.bfloat16)
    (near,) = project(contexts, own, place, 0, 1, jnp.float32)
    far = {d: along_x(far[d - 1], d) for d in (2, 1, 3)}
    out_width = model // 8
    residual = lax.dynamic_slice_in_dim(targets, (segment * 4 + x) * out_width, out_width, 1)
    summed = residual.astype(jnp.float32) + near
    for d in (1, 2, 3):
        summed = summed + far[d].astype(jnp.float32)
    return summed.astype(jnp.bfloat16)


def solution(mesh):
    placed = (
        P("ctx", None),
        P("ctx", None),
        P("ctx"),
        P("segment", None),
        P("segment", None, None, "mp"),
    )
    return jax.shard_map(
        local, mesh=mesh, in_specs=placed, out_specs=P("ctx", ("segment", "mp")), check_vma=False
    )
```

```python
import functools

import jax
import jax.numpy as jnp
from jax import lax
from jax.experimental import pallas as pl
from jax.experimental.pallas import tpu as pltpu
from jax.sharding import PartitionSpec as P

HEADS = 16
AXES = ("segment", "ctx", "mp")
MARK_ROWS = 16
DEAD = -1e30
VMEM = 56 * 2**20
ATTEND_VMEM = 40 * 2**20
LIGHT = pl.CostEstimate(flops=0, bytes_accessed=1024, transcendentals=0)


def device_of(x, y, z, core):
    return (z // 2) * 64 + (z % 2) * 32 + y * 8 + core * 4 + x


def place_of(i):
    return i % 4, (i // 8) % 4, (i // 64) * 2 + (i // 32) % 2, (i // 4) % 2


def moved(block, step, senders=lambda x, y, z, core: True):
    route = []
    for i in range(128):
        place = place_of(i)
        if senders(*place):
            x, y, z, core = step(*place)
            route.append((i, device_of(x % 4, y % 4, z % 4, core % 2)))
    return lax.ppermute(block, AXES, route)


def along_x(block, d):
    return moved(block, lambda x, y, z, c: (x + d, y, z, c))


def along_y(block, d, senders=lambda x, y, z, core: True):
    return moved(block, lambda x, y, z, c: (x, y + d, z, c), senders)


def along_z(block, d):
    return moved(block, lambda x, y, z, c: (x, y, z + d, c))


def other_core(block, senders=lambda x, y, z, core: True):
    return moved(block, lambda x, y, z, c: (x, y, z, c + 1), senders)


def norm_rows(hidden_rows, gain_row):
    widened = hidden_rows.astype(jnp.float32)
    inverse = lax.rsqrt(jnp.mean(widened * widened, axis=-1, keepdims=True) + 1e-06)
    return (widened * inverse * gain_row).astype(jnp.bfloat16)


def section_kernel(info_ref, memory, targets, gain_ref, w_ref, *refs):
    *out_refs, normed, x_rows, total, arrival = refs
    k, steps = pl.program_id(0), pl.num_programs(0)
    depth, width = w_ref.shape[1], w_ref.shape[3]
    rows = total.shape[0]
    half = rows // 2
    dim = out_refs[0].shape[1]
    encoder = info_ref[0] < 2

    def normalise(source, count):
        copy = pltpu.make_async_copy(source, x_rows.at[pl.ds(0, count)], arrival)
        copy.start()
        copy.wait()
        for top in range(0, count, 64):
            part = norm_rows(x_rows[pl.ds(top, 64), :], gain_ref[...])
            for j in range(normed.shape[0]):
                normed[j, pl.ds(top, 64), :] = part[:, j * depth : (j + 1) * depth]

    @pl.when((k == 0) & encoder)
    def _():
        normalise(memory, half)

    @pl.when((k == 0) & jnp.logical_not(encoder))
    def _():
        normalise(targets, rows)

    def add(rows_of, found):
        @pl.when(k == 0)
        def _():
            total[rows_of, :] = found

        @pl.when(k > 0)
        def _():
            total[rows_of, :] += found

    @pl.when(encoder)
    def _():
        both = w_ref[0].reshape(depth, 2 * width)
        found = jnp.dot(normed[k, :half, :], both, preferred_element_type=jnp.float32)
        add(pl.ds(0, half), found[:, :width])
        add(pl.ds(half, half), found[:, width:])

    @pl.when(jnp.logical_not(encoder))
    def _():
        both = w_ref[0].reshape(depth, 2 * width)
        found = jnp.dot(normed[k], both[:, :width], preferred_element_type=jnp.float32)
        add(pl.ds(0, rows), found)

    @pl.when(k == steps - 1)
    def _():
        position = lax.broadcasted_iota(jnp.int32, (MARK_ROWS, dim), 1)
        marks = jnp.where(position < half - info_ref[1], 0.0, DEAD).astype(jnp.bfloat16)
        for d, ref in enumerate(out_refs):
            head = (info_ref[0] + d) % 4
            ref[:rows, :] = total[:, pl.ds(pl.multiple_of(head * dim, dim), dim)].astype(jnp.bfloat16)
            ref[rows:, :] = marks


def section(info, memory, targets, gains, weights, dim):
    rows, model = targets.shape
    width = weights.shape[3]
    depth = 1024
    steps = model // depth
    slab = (rows + MARK_ROWS, dim)
    anywhere = pl.BlockSpec(memory_space=pl.ANY)
    return pl.pallas_call(
        section_kernel,
        grid_spec=pltpu.PrefetchScalarGridSpec(
            num_scalar_prefetch=1,
            grid=(steps,),
            in_specs=[
                anywhere,
                anywhere,
                pl.BlockSpec((1, model), lambda k, info: (0, 0)),
                pl.BlockSpec((1, depth, 2, width), lambda k, info: (0, k, 0, 0)),
            ],
            out_specs=[pl.BlockSpec(slab, lambda k, info: (0, 0))] * 4,
            scratch_shapes=[
                pltpu.VMEM((steps, rows, depth), jnp.bfloat16),
                pltpu.VMEM((rows, model), jnp.bfloat16),
                pltpu.VMEM((rows, width), jnp.float32),
                pltpu.SemaphoreType.DMA,
            ],
        ),
        out_shape=[jax.ShapeDtypeStruct(slab, jnp.bfloat16)] * 4,
        cost_estimate=LIGHT,
        compiler_params=pltpu.CompilerParams(vmem_limit_bytes=VMEM),
    )(info, memory, targets, gains, weights)


def second_half_kernel(start_ref, w_ref, *out_refs):
    depth, width = w_ref.shape[1], w_ref.shape[3]
    found = w_ref[0].reshape(depth, 2 * width)[:, width:]
    for j, ref in enumerate(out_refs):
        size = ref.shape[0]
        ref[...] = found[j * size : (j + 1) * size]


def second_half(weights, start, depth, steps, pieces):
    width = weights.shape[3]
    return pl.pallas_call(
        second_half_kernel,
        grid_spec=pltpu.PrefetchScalarGridSpec(
            num_scalar_prefetch=1,
            grid=(steps,),
            in_specs=[pl.BlockSpec((1, depth, 2, width), lambda k, start: (0, start[0] + k, 0, 0))],
            out_specs=[pl.BlockSpec((depth // pieces, width), lambda k, start: (k, 0))] * pieces,
        ),
        out_shape=[jax.ShapeDtypeStruct((steps * depth // pieces, width), jnp.bfloat16)] * pieces,
        cost_estimate=LIGHT,
        compiler_params=pltpu.CompilerParams(vmem_limit_bytes=VMEM),
    )(start.reshape(1), weights)


def attend_kernel(first, half, chunk, chunks, z_ref, *refs):
    if first:
        *slabs, acc_ref, peak_ref, total_ref, queries, keys, values, marks = refs
    else:
        *slabs, acc_ref, peak_ref, total_ref, out_a, out_b, queries, keys, values, marks = refs
    q_slabs, blocks = slabs[:4], slabs[4:]
    size = (blocks[0].shape[1] - MARK_ROWS) // 2
    z = z_ref[0]
    pieces = [ref.at[n] for ref in blocks for n in range(ref.shape[0])]
    for j, ref in enumerate(pieces):
        keys[j * size : (j + 1) * size, :] = ref[:size, :]
        values[j * size : (j + 1) * size, :] = ref[size : 2 * size, :]
        marks[:, j * size : (j + 1) * size] = ref[2 * size : 2 * size + 8, :].astype(jnp.float32)

    def run(at):
        base = at * 2 * half

        def take(index, when, top):
            @pl.when(when)
            def _():
                queries[pl.ds(top, half), :] = q_slabs[index][at * half : (at + 1) * half, :]

        take(2, z < 2, 0)
        take(0, z >= 2, 0)
        inner = (z == 1) | (z == 2)
        take(3, inner, half)
        take(1, jnp.logical_not(inner), half)

        part = 256
        for top in range(0, 2 * half, part):
            scores = lax.dot_general(
                queries[top : top + part, :],
                keys[...],
                (((1,), (1,)), ((), ())),
                preferred_element_type=jnp.float32,
            )
            scores = scores + marks[0:1, :]
            peak = jnp.max(scores, axis=1, keepdims=True)
            mine = slice(base + top, base + top + part)
            if not first:
                before = peak_ref[mine, :1]
                peak = jnp.maximum(peak, before)
                scale = jnp.exp(before - peak)
            soft = jnp.exp(scores - peak)
            total = jnp.sum(soft, axis=1, keepdims=True)
            mixed = jnp.dot(
                soft.astype(jnp.bfloat16), values[...], preferred_element_type=jnp.float32
            )
            if first:
                acc_ref[mine, :] = mixed
                peak_ref[mine, :] = jnp.broadcast_to(peak, (part, 128))
                total_ref[mine, :] = jnp.broadcast_to(total, (part, 128))
            else:
                mixed = mixed + scale * acc_ref[mine, :]
                total = total + scale * total_ref[mine, :1]
                found = (mixed / total).astype(jnp.bfloat16)
                if top < half:
                    out_a[top : top + part, :] = found
                else:
                    out_b[top - half : top - half + part, :] = found

    for at in range(chunks) if first else (chunk,):
        run(at)


def attend(z, q_slabs, blocks, chunks, state=None, chunk=0):
    rows, dim = q_slabs[0].shape[0] - MARK_ROWS, q_slabs[0].shape[1]
    half = rows // chunks
    first = state is None
    keys = sum(b.shape[0] for b in blocks) * (blocks[0].shape[1] - MARK_ROWS) // 2
    vmem = pl.BlockSpec(memory_space=pltpu.VMEM)
    if first:
        out_shape = [jax.ShapeDtypeStruct((2 * rows, last), jnp.float32) for last in (dim, 128, 128)]
    else:
        out_shape = [jax.ShapeDtypeStruct((half, dim), jnp.bfloat16)] * 2
    operands = [*q_slabs, *blocks, *(() if first else state)]
    return pl.pallas_call(
        functools.partial(attend_kernel, first, half, chunk, chunks),
        in_specs=[pl.BlockSpec(memory_space=pltpu.SMEM)] + [vmem] * len(operands),
        out_specs=[vmem] * len(out_shape),
        scratch_shapes=[
            pltpu.VMEM((2 * half, dim), jnp.bfloat16),
            pltpu.VMEM((keys, dim), jnp.bfloat16),
            pltpu.VMEM((keys, dim), jnp.bfloat16),
            pltpu.VMEM((8, keys), jnp.float32),
        ],
        out_shape=out_shape,
        cost_estimate=LIGHT,
        compiler_params=pltpu.CompilerParams(vmem_limit_bytes=ATTEND_VMEM),
    )(z.reshape(1), *operands)


def project_kernel(first, place_ref, c0, c1, c2, c3, *refs):
    sources, rest = refs[:5], refs[5:]
    *out_refs, held, context, arrived = rest
    z, x, core, held_set = place_ref[0], place_ref[1], place_ref[2], place_ref[3]
    dim, width = c0.shape[1], held.shape[1]
    for d, ref in enumerate((c0, c1, c2, c3)):
        head = (z + 4 - d) % 4
        context[:, pl.ds(pl.multiple_of(head * dim, dim), dim)] = ref[...]

    def fetch(j, action):
        wanted = (x + first + j) % 4
        kind = jnp.where(wanted // 2 == core, 0, 2) + jnp.where(wanted % 2 == held_set, 0, 1)

        @pl.when(z >= 2)
        def _():
            top = pl.multiple_of(wanted * width, width)
            action(pltpu.make_async_copy(sources[4].at[pl.ds(top, width)], held.at[j], arrived.at[j]))

        for n in range(4):

            @pl.when((z < 2) & (kind == n))
            def _(n=n):
                action(pltpu.make_async_copy(sources[n], held.at[j], arrived.at[j]))

    for j in range(len(out_refs)):
        fetch(j, lambda copy: copy.start())
    for j, ref in enumerate(out_refs):
        fetch(j, lambda copy: copy.wait())
        mixed = lax.dot_general(
            context[...], held[j], (((1,), (1,)), ((), ())), preferred_element_type=jnp.float32
        )
        ref[...] = mixed.astype(ref.dtype)


def project(place, contexts, sources, first, count, dtype):
    rows, dim = contexts[0].shape
    width = sources[4].shape[0] // 4
    vmem = pl.BlockSpec(memory_space=pltpu.VMEM)
    return pl.pallas_call(
        functools.partial(project_kernel, first),
        in_specs=[pl.BlockSpec(memory_space=pltpu.SMEM)]
        + [vmem] * 4
        + [pl.BlockSpec(memory_space=pl.ANY)] * 5,
        out_specs=[vmem] * count,
        out_shape=[jax.ShapeDtypeStruct((rows, width), dtype)] * count,
        scratch_shapes=[
            pltpu.VMEM((count, width, 4 * dim), jnp.bfloat16),
            pltpu.VMEM((rows, 4 * dim), jnp.bfloat16),
            pltpu.SemaphoreType.DMA((count,)),
        ],
        cost_estimate=LIGHT,
        compiler_params=pltpu.CompilerParams(vmem_limit_bytes=VMEM),
    )(place, *contexts, *sources)


def after(value, *others):
    return lax.optimization_barrier((value, *others))[0]


def local(targets, memory, pad_counts, norm_gains, proj_weights):
    segment, ctx, x = (lax.axis_index(axis) for axis in AXES)
    core, y, low = ctx % 2, (ctx // 2) % 4, ctx // 8
    z = 2 * segment + low
    model, width = proj_weights.shape[1], proj_weights.shape[3]
    dim = width * 4 // HEADS
    rows = targets.shape[0]
    half = model // 2
    chunks = 2
    down = lambda x, y, z, c: (x, y, 3 - z, c)
    encoder = lambda x, y, z, c: z < 2
    decoder = lambda x, y, z, c: z >= 2
    flip = lambda x, y, z, c: (x, y, 1 - z, c)
    is_encoder = segment == 0

    info = jnp.stack([z, pad_counts[0]])
    own, *to = section(info, memory, targets, norm_gains, proj_weights, dim)
    r1, r3, r2 = along_z(to[0], 1), along_z(to[2], 3), along_z(to[1], 2)

    held_set = (low + y) % 2
    (share,) = second_half(after(proj_weights, own), core * 2 + 1 - held_set, half // 4, 1, 1)
    p = moved(share, down, decoder)

    early = jnp.where(is_encoder, own, jnp.where(z == 2, r1, r3))
    late = jnp.where(z == 0, r3, jnp.where(z == 1, r1, r2))
    pair = jnp.stack([after(early, share), late])
    y1, y3 = along_y(pair, 1), along_y(pair, 3)
    (mine,) = second_half(after(proj_weights, pair), jnp.int32(2), half // 2, 2, 1)
    y1, y3, mine, p = lax.optimization_barrier((y1, y3, mine, p))
    far0, far1 = along_y(y1[0], 1), along_y(y3[1], 3)
    slabs = [own, r1, r2, r3]
    blocks = [pair, y1, y3]
    state = attend(z, slabs, blocks + [other_core(b) for b in blocks], chunks)

    quarter = half // 8
    far0, far1, *state = lax.optimization_barrier((far0, far1, *state))
    sz = moved(p[:quarter], flip, encoder)
    sy = moved(p[quarter:], lambda x, y, z, c: (x, y ^ 1, z, c), encoder)
    blocks = [far0[None], far1[None]]
    blocks = blocks + [other_core(b) for b in blocks]
    place = jnp.stack([z, x, core, held_set])

    first_part = attend(z, slabs, blocks, chunks, state, 0)
    second_part = attend(after(z, first_part[0]), slabs, blocks, chunks, state, 1)
    moving = []
    for ca, cb in (first_part, second_part):
        moving.append([ca, along_z(cb, 1), along_z(ca, 2), along_z(cb, 3)])
    twin = other_core(after(p, state[0]), encoder)
    moving[0], sz, sy, _ = lax.optimization_barrier((moving[0], sz, sy, second_part[0]))
    s = jnp.concatenate([sz, sy])
    sources = [p, s, twin, other_core(s, encoder), mine]
    finished = []
    out_width = model // 8
    residual = lax.dynamic_slice_in_dim(targets, (segment * 4 + x) * out_width, out_width, 1)
    for chunk, contexts in enumerate(moving):
        far = project(place, contexts, sources, 1, 3, jnp.bfloat16)
        (near,) = project(place, contexts, sources, 0, 1, jnp.float32)
        part = rows // chunks
        summed = residual[chunk * part : (chunk + 1) * part].astype(jnp.float32) + near
        for d in (1, 3, 2):
            summed = summed + along_x(far[d - 1], d).astype(jnp.float32)
        finished.append(summed.astype(jnp.bfloat16))
    return jnp.concatenate(finished)


def solution(mesh):
    placed = (
        P("ctx", None),
        P("ctx", None),
        P("ctx"),
        P("segment", None),
        P("segment", None, None, "mp"),
    )
    return jax.shard_map(
        local, mesh=mesh, in_specs=placed, out_specs=P("ctx", ("segment", "mp")), check_vma=False
    )
```

```python
import functools

import jax
import jax.numpy as jnp
from jax import lax
from jax.experimental import pallas as pl
from jax.experimental.pallas import tpu as pltpu
from jax.sharding import PartitionSpec as P

HEADS = 16
AXES = ("segment", "ctx", "mp")
MARK_ROWS = 16
DEAD = -1e30
VMEM = 56 * 2**20
ATTEND_VMEM = 40 * 2**20
LIGHT = pl.CostEstimate(flops=0, bytes_accessed=1024, transcendentals=0)


def device_of(x, y, z, core):
    return (z // 2) * 64 + (z % 2) * 32 + y * 8 + core * 4 + x


def place_of(i):
    return i % 4, (i // 8) % 4, (i // 64) * 2 + (i // 32) % 2, (i // 4) % 2


def moved(block, step, senders=lambda x, y, z, core: True):
    route = []
    for i in range(128):
        place = place_of(i)
        if senders(*place):
            x, y, z, core = step(*place)
            route.append((i, device_of(x % 4, y % 4, z % 4, core % 2)))
    return lax.ppermute(block, AXES, route)


def along_x(block, d):
    return moved(block, lambda x, y, z, c: (x + d, y, z, c))


def along_y(block, d, senders=lambda x, y, z, core: True):
    return moved(block, lambda x, y, z, c: (x, y + d, z, c), senders)


def along_z(block, d):
    return moved(block, lambda x, y, z, c: (x, y, z + d, c))


def other_core(block, senders=lambda x, y, z, core: True):
    return moved(block, lambda x, y, z, c: (x, y, z, c + 1), senders)


def norm_rows(hidden_rows, gain_row):
    widened = hidden_rows.astype(jnp.float32)
    inverse = lax.rsqrt(jnp.mean(widened * widened, axis=-1, keepdims=True) + 1e-06)
    return (widened * inverse * gain_row).astype(jnp.bfloat16)


def section_kernel(z_ref, pad_ref, memory, targets, gain_ref, w_ref, *refs):
    *out_refs, normed, x_rows, total, arrival = refs
    k, steps = pl.program_id(0), pl.num_programs(0)
    depth, width = w_ref.shape[1], w_ref.shape[3]
    rows = total.shape[0]
    half = rows // 2
    dim = out_refs[0].shape[1]
    encoder = z_ref[0] < 2

    def normalise(source, count):
        block = 128
        copies = [
            pltpu.make_async_copy(
                source.at[pl.ds(top, block)], x_rows.at[pl.ds(top, block)], arrival.at[top // block]
            )
            for top in range(0, count, block)
        ]
        for copy in copies:
            copy.start()
        for top in range(0, count, 64):
            if top % block == 0:
                copies[top // block].wait()
            part = norm_rows(x_rows[pl.ds(top, 64), :], gain_ref[...])
            for j in range(normed.shape[0]):
                normed[j, pl.ds(top, 64), :] = part[:, j * depth : (j + 1) * depth]

    @pl.when((k == 0) & encoder)
    def _():
        normalise(memory, half)

    @pl.when((k == 0) & jnp.logical_not(encoder))
    def _():
        normalise(targets, rows)

    def add(rows_of, found):
        @pl.when(k == 0)
        def _():
            total[rows_of, :] = found

        @pl.when(k > 0)
        def _():
            total[rows_of, :] += found

    @pl.when(encoder)
    def _():
        both = w_ref[0].reshape(depth, 2 * width)
        found = jnp.dot(normed[k, :half, :], both, preferred_element_type=jnp.float32)
        add(pl.ds(0, half), found[:, :width])
        add(pl.ds(half, half), found[:, width:])

    @pl.when(jnp.logical_not(encoder))
    def _():
        both = w_ref[0].reshape(depth, 2 * width)
        found = jnp.dot(normed[k], both[:, :width], preferred_element_type=jnp.float32)
        add(pl.ds(0, rows), found)

    @pl.when(k == steps - 1)
    def _():
        position = lax.broadcasted_iota(jnp.int32, (MARK_ROWS, dim), 1)
        marks = jnp.where(position < half - pad_ref[0], 0.0, DEAD).astype(jnp.bfloat16)
        for d, ref in enumerate(out_refs):
            head = (z_ref[0] + d) % 4
            ref[:rows, :] = total[:, pl.ds(pl.multiple_of(head * dim, dim), dim)].astype(jnp.bfloat16)
            ref[rows:, :] = marks


def section(z, pad_counts, memory, targets, gains, weights, dim):
    rows, model = targets.shape
    width = weights.shape[3]
    depth = 1024
    steps = model // depth
    slab = (rows + MARK_ROWS, dim)
    anywhere = pl.BlockSpec(memory_space=pl.ANY)
    return pl.pallas_call(
        section_kernel,
        grid_spec=pltpu.PrefetchScalarGridSpec(
            num_scalar_prefetch=2,
            grid=(steps,),
            in_specs=[
                anywhere,
                anywhere,
                pl.BlockSpec((1, model), lambda k, z, pad: (0, 0)),
                pl.BlockSpec((1, depth, 2, width), lambda k, z, pad: (0, k, 0, 0)),
            ],
            out_specs=[pl.BlockSpec(slab, lambda k, z, pad: (0, 0))] * 4,
            scratch_shapes=[
                pltpu.VMEM((steps, rows, depth), jnp.bfloat16),
                pltpu.VMEM((rows, model), jnp.bfloat16),
                pltpu.VMEM((rows, width), jnp.float32),
                pltpu.SemaphoreType.DMA((rows // 128,)),
            ],
        ),
        out_shape=[jax.ShapeDtypeStruct(slab, jnp.bfloat16)] * 4,
        cost_estimate=LIGHT,
        compiler_params=pltpu.CompilerParams(vmem_limit_bytes=VMEM),
    )(z.reshape(1), pad_counts, memory, targets, gains, weights)


def second_half_kernel(start_ref, w_ref, *out_refs):
    depth, width = w_ref.shape[1], w_ref.shape[3]
    found = w_ref[0].reshape(depth, 2 * width)[:, width:]
    for j, ref in enumerate(out_refs):
        size = ref.shape[0]
        ref[...] = found[j * size : (j + 1) * size]


def second_half(weights, start, depth, steps, pieces):
    width = weights.shape[3]
    return pl.pallas_call(
        second_half_kernel,
        grid_spec=pltpu.PrefetchScalarGridSpec(
            num_scalar_prefetch=1,
            grid=(steps,),
            in_specs=[pl.BlockSpec((1, depth, 2, width), lambda k, start: (0, start[0] + k, 0, 0))],
            out_specs=[pl.BlockSpec((depth // pieces, width), lambda k, start: (k, 0))] * pieces,
        ),
        out_shape=[jax.ShapeDtypeStruct((steps * depth // pieces, width), jnp.bfloat16)] * pieces,
        cost_estimate=LIGHT,
        compiler_params=pltpu.CompilerParams(vmem_limit_bytes=VMEM),
    )(start.reshape(1), weights)


def attend_kernel(first, half, chunks, z_ref, *refs):
    if first:
        *slabs, acc_ref, peak_ref, total_ref, queries, keys, values, marks = refs
    else:
        *slabs, acc_ref, peak_ref, total_ref, out_a, out_b, queries, keys, values, marks = refs
    q_slabs, blocks = slabs[:4], slabs[4:]
    size = (blocks[0].shape[1] - MARK_ROWS) // 2
    z = z_ref[0]
    pieces = [ref.at[n] for ref in blocks for n in range(ref.shape[0])]
    for j, ref in enumerate(pieces):
        keys[j * size : (j + 1) * size, :] = ref[:size, :]
        values[j * size : (j + 1) * size, :] = ref[size : 2 * size, :]
        marks[:, j * size : (j + 1) * size] = ref[2 * size : 2 * size + 8, :].astype(jnp.float32)

    def run(at):
        base = at * 2 * half

        def take(index, when, top):
            @pl.when(when)
            def _():
                queries[pl.ds(top, half), :] = q_slabs[index][at * half : (at + 1) * half, :]

        take(2, z < 2, 0)
        take(0, z >= 2, 0)
        inner = (z == 1) | (z == 2)
        take(3, inner, half)
        take(1, jnp.logical_not(inner), half)

        part = 256
        for top in range(0, 2 * half, part):
            scores = lax.dot_general(
                queries[top : top + part, :],
                keys[...],
                (((1,), (1,)), ((), ())),
                preferred_element_type=jnp.float32,
            )
            scores = scores + marks[0:1, :]
            peak = jnp.max(scores, axis=1, keepdims=True)
            mine = slice(base + top, base + top + part)
            if not first:
                before = peak_ref[mine, :1]
                peak = jnp.maximum(peak, before)
                scale = jnp.exp(before - peak)
            soft = jnp.exp(scores - peak)
            total = jnp.sum(soft, axis=1, keepdims=True)
            mixed = jnp.dot(
                soft.astype(jnp.bfloat16), values[...], preferred_element_type=jnp.float32
            )
            if first:
                acc_ref[mine, :] = mixed
                peak_ref[mine, :] = jnp.broadcast_to(peak, (part, 128))
                total_ref[mine, :] = jnp.broadcast_to(total, (part, 128))
            else:
                mixed = mixed + scale * acc_ref[mine, :]
                total = total + scale * total_ref[mine, :1]
                found = (mixed / total).astype(jnp.bfloat16)
                if top < half:
                    out_a[at * half + top : at * half + top + part, :] = found
                else:
                    out_b[at * half + top - half : at * half + top - half + part, :] = found

    for at in range(chunks):
        run(at)


def attend(z, q_slabs, blocks, chunks, state=None):
    rows, dim = q_slabs[0].shape[0] - MARK_ROWS, q_slabs[0].shape[1]
    half = rows // chunks
    first = state is None
    keys = sum(b.shape[0] for b in blocks) * (blocks[0].shape[1] - MARK_ROWS) // 2
    vmem = pl.BlockSpec(memory_space=pltpu.VMEM)
    if first:
        out_shape = [jax.ShapeDtypeStruct((2 * rows, last), jnp.float32) for last in (dim, 128, 128)]
    else:
        out_shape = [jax.ShapeDtypeStruct((rows, dim), jnp.bfloat16)] * 2
    operands = [*q_slabs, *blocks, *(() if first else state)]
    return pl.pallas_call(
        functools.partial(attend_kernel, first, half, chunks),
        in_specs=[pl.BlockSpec(memory_space=pltpu.SMEM)] + [vmem] * len(operands),
        out_specs=[vmem] * len(out_shape),
        scratch_shapes=[
            pltpu.VMEM((2 * half, dim), jnp.bfloat16),
            pltpu.VMEM((keys, dim), jnp.bfloat16),
            pltpu.VMEM((keys, dim), jnp.bfloat16),
            pltpu.VMEM((8, keys), jnp.float32),
        ],
        out_shape=out_shape,
        cost_estimate=LIGHT,
        compiler_params=pltpu.CompilerParams(vmem_limit_bytes=ATTEND_VMEM),
    )(z.reshape(1), *operands)


def project_kernel(first, z_ref, x_ref, core_ref, set_ref, c0, c1, c2, c3, *refs):
    sources, mine = refs[:8], refs[8]
    *out_refs, held, context, arrived = refs[9:]
    z, x, core, held_set = z_ref[0], x_ref[0], core_ref[0], set_ref[0]
    dim, width = c0.shape[1], held.shape[1]
    part = width // 2

    def fetch(j, action):
        wanted = (x + first + j) % 4
        slot, arrival = held.at[j], arrived.at[j]

        @pl.when(z >= 2)
        def _():
            top = pl.multiple_of(wanted * width, width)
            action(pltpu.make_async_copy(mine.at[pl.ds(top, width)], slot, arrival))

        for n in range(4):

            @pl.when((z < 2) & ((wanted + 4 - held_set) % 4 == n))
            def _(n=n):
                for source, side in ((sources[n], core), (sources[4 + n], 1 - core)):
                    top = pl.multiple_of(side * part, part)
                    action(pltpu.make_async_copy(source, slot.at[pl.ds(top, part)], arrival))

    for j in range(len(out_refs)):
        fetch(j, lambda copy: copy.start())
    for d, ref in enumerate((c0, c1, c2, c3)):
        head = (z + 4 - d) % 4
        context[:, pl.ds(pl.multiple_of(head * dim, dim), dim)] = ref[...]
    for j, ref in enumerate(out_refs):
        fetch(j, lambda copy: copy.wait())
        mixed = lax.dot_general(
            context[...], held[j], (((1,), (1,)), ((), ())), preferred_element_type=jnp.float32
        )
        ref[...] = mixed.astype(ref.dtype)


def project(place, contexts, sources, first, count, dtype):
    rows, dim = contexts[0].shape
    width = sources[-1].shape[0] // 4
    vmem = pl.BlockSpec(memory_space=pltpu.VMEM)
    return pl.pallas_call(
        functools.partial(project_kernel, first),
        in_specs=[pl.BlockSpec(memory_space=pltpu.SMEM)] * 4
        + [vmem] * 4
        + [pl.BlockSpec(memory_space=pl.ANY)] * 9,
        out_specs=[vmem] * count,
        out_shape=[jax.ShapeDtypeStruct((rows, width), dtype)] * count,
        scratch_shapes=[
            pltpu.VMEM((count, width, 4 * dim), jnp.bfloat16),
            pltpu.VMEM((rows, 4 * dim), jnp.bfloat16),
            pltpu.SemaphoreType.DMA((count,)),
        ],
        cost_estimate=LIGHT,
        compiler_params=pltpu.CompilerParams(vmem_limit_bytes=VMEM),
    )(*(scalar.reshape(1) for scalar in place), *contexts, *sources)


def after(value, *others):
    return lax.optimization_barrier((value, *others))[0]


def local(targets, memory, pad_counts, norm_gains, proj_weights):
    segment, ctx, x = (lax.axis_index(axis) for axis in AXES)
    core, y, low = ctx % 2, (ctx // 2) % 4, ctx // 8
    z = 2 * segment + low
    model, width = proj_weights.shape[1], proj_weights.shape[3]
    dim = width * 4 // HEADS
    rows = targets.shape[0]
    half = model // 2
    chunks = 2
    down = lambda x, y, z, c: (x, y, 3 - z, c)
    encoder = lambda x, y, z, c: z < 2
    decoder = lambda x, y, z, c: z >= 2
    flip = lambda x, y, z, c: (x, y, 1 - z, c)
    is_encoder = segment == 0

    held_set = (y + 2 * low) % 4
    wanted_set = (y + 2 * (1 - low)) % 4
    (share,) = second_half(proj_weights, wanted_set * 2 + core, half // 8, 1, 1)
    p = moved(share, down, decoder)

    own, *to = section(after(z, share), pad_counts, memory, targets, norm_gains, proj_weights, dim)
    own, to, p = lax.optimization_barrier((own, to, p))
    above, below = along_y(p, 3, encoder), along_y(p, 1, encoder)
    r1, r3, r2 = along_z(to[0], 1), along_z(to[2], 3), along_z(to[1], 2)
    early = jnp.where(is_encoder, own, jnp.where(z == 2, r1, r3))
    late = jnp.where(z == 0, r3, jnp.where(z == 1, r1, r2))
    pair = jnp.stack([early, late])
    above_twin = other_core(above, encoder)

    pair, p, above, below, above_twin = lax.optimization_barrier((pair, p, above, below, above_twin))
    y1, y3 = along_y(pair, 1), along_y(pair, 3)
    across = moved(p, flip, encoder)
    twin, below_twin = other_core(p, encoder), other_core(below, encoder)
    (mine,) = second_half(after(proj_weights, pair), jnp.int32(2), half // 2, 2, 1)

    y1, y3, twin, below_twin, mine = lax.optimization_barrier((y1, y3, twin, below_twin, mine))
    far0, far1 = along_y(y1[0], 1), along_y(y3[1], 3)
    slabs = [own, r1, r2, r3]
    blocks = [pair, y1, y3]
    state = attend(z, slabs, blocks + [other_core(b) for b in blocks], chunks)

    far0, far1, across, *state = lax.optimization_barrier((far0, far1, across, *state))
    across_twin = other_core(across, encoder)
    blocks = [far0[None], far1[None]]
    blocks = blocks + [other_core(b) for b in blocks]
    ca, cb = attend(z, slabs, blocks, chunks, state)
    contexts = [ca, along_z(cb, 1), along_z(ca, 2), along_z(cb, 3)]
    sources = [p, above, across, below, twin, above_twin, across_twin, below_twin, mine]
    place = [z, x, core, held_set]
    out_width = model // 8
    residual = lax.dynamic_slice_in_dim(targets, (segment * 4 + x) * out_width, out_width, 1)
    far = project(place, contexts, sources, 1, 3, jnp.bfloat16)
    (near,) = project([after(z, far[0]), *place[1:]], contexts, sources, 0, 1, jnp.float32)
    far = {d: along_x(far[d - 1], d) for d in (2, 1, 3)}
    summed = lax.optimization_barrier(residual.astype(jnp.float32) + near + far[2].astype(jnp.float32))
    return (summed + far[1].astype(jnp.float32) + far[3].astype(jnp.float32)).astype(jnp.bfloat16)


def solution(mesh):
    placed = (
        P("ctx", None),
        P("ctx", None),
        P("ctx"),
        P("segment", None),
        P("segment", None, None, "mp"),
    )
    return jax.shard_map(
        local, mesh=mesh, in_specs=placed, out_specs=P("ctx", ("segment", "mp")), check_vma=False
    )
```

```python
import functools

import jax
import jax.numpy as jnp
from jax import lax
from jax.experimental import pallas as pl
from jax.experimental.pallas import tpu as pltpu
from jax.sharding import PartitionSpec as P

HEADS = 16
AXES = ("segment", "ctx", "mp")
MARK_ROWS = 16
DEAD = -1e30
VMEM = 56 * 2**20
ATTEND_VMEM = 40 * 2**20
SMALL_VMEM = 24 * 2**20
LIGHT = pl.CostEstimate(flops=0, bytes_accessed=1024, transcendentals=0)


def device_of(x, y, z, core):
    return (z // 2) * 64 + (z % 2) * 32 + y * 8 + core * 4 + x


def place_of(i):
    return i % 4, (i // 8) % 4, (i // 64) * 2 + (i // 32) % 2, (i // 4) % 2


def moved(block, step, senders=lambda x, y, z, core: True):
    route = []
    for i in range(128):
        place = place_of(i)
        if senders(*place):
            x, y, z, core = step(*place)
            route.append((i, device_of(x % 4, y % 4, z % 4, core % 2)))
    return lax.ppermute(block, AXES, route)


def along_x(block, d):
    return moved(block, lambda x, y, z, c: (x + d, y, z, c))


def along_y(block, d, senders=lambda x, y, z, core: True):
    return moved(block, lambda x, y, z, c: (x, y + d, z, c), senders)


def along_z(block, d):
    return moved(block, lambda x, y, z, c: (x, y, z + d, c))


def other_core(block, senders=lambda x, y, z, core: True):
    return moved(block, lambda x, y, z, c: (x, y, z, c + 1), senders)


def norm_rows(hidden_rows, gain_row):
    widened = hidden_rows.astype(jnp.float32)
    inverse = lax.rsqrt(jnp.mean(widened * widened, axis=-1, keepdims=True) + 1e-06)
    return (widened * inverse * gain_row).astype(jnp.bfloat16)


def section_kernel(pad_ref, memory, targets, gain_ref, w_ref, *refs):
    *out_refs, normed, x_rows, total, arrival = refs
    k, steps = pl.program_id(0), pl.num_programs(0)
    depth, width = w_ref.shape[1], w_ref.shape[3]
    rows = total.shape[0]
    half = rows // 2
    dim = out_refs[0].shape[1]
    z = position()[2]
    encoder = z < 2

    def normalise(source, count):
        block = 128
        copies = [
            pltpu.make_async_copy(
                source.at[pl.ds(top, block)], x_rows.at[pl.ds(top, block)], arrival.at[top // block]
            )
            for top in range(0, count, block)
        ]
        for copy in copies:
            copy.start()
        for top in range(0, count, 64):
            if top % block == 0:
                copies[top // block].wait()
            part = norm_rows(x_rows[pl.ds(top, 64), :], gain_ref[...])
            for j in range(normed.shape[0]):
                normed[j, pl.ds(top, 64), :] = part[:, j * depth : (j + 1) * depth]

    @pl.when((k == 0) & encoder)
    def _():
        normalise(memory, half)

    @pl.when((k == 0) & jnp.logical_not(encoder))
    def _():
        normalise(targets, rows)

    def add(rows_of, found):
        @pl.when(k == 0)
        def _():
            total[rows_of, :] = found

        @pl.when(k > 0)
        def _():
            total[rows_of, :] += found

    @pl.when(encoder)
    def _():
        both = w_ref[0].reshape(depth, 2 * width)
        found = jnp.dot(normed[k, :half, :], both, preferred_element_type=jnp.float32)
        add(pl.ds(0, half), found[:, :width])
        add(pl.ds(half, half), found[:, width:])

    @pl.when(jnp.logical_not(encoder))
    def _():
        both = w_ref[0].reshape(depth, 2 * width)
        found = jnp.dot(normed[k], both[:, :width], preferred_element_type=jnp.float32)
        add(pl.ds(0, rows), found)

    @pl.when(k == steps - 1)
    def _():
        position = lax.broadcasted_iota(jnp.int32, (MARK_ROWS, dim), 1)
        marks = jnp.where(position < half - pad_ref[0], 0.0, DEAD).astype(jnp.bfloat16)
        for d, ref in enumerate(out_refs):
            head = (z + d) % 4
            ref[:rows, :] = total[:, pl.ds(pl.multiple_of(head * dim, dim), dim)].astype(jnp.bfloat16)
            ref[rows:, :] = marks


def section(pad_counts, memory, targets, gains, weights, dim):
    rows, model = targets.shape
    width = weights.shape[3]
    depth = 1024
    steps = model // depth
    slab = (rows + MARK_ROWS, dim)
    anywhere = pl.BlockSpec(memory_space=pl.ANY)
    return pl.pallas_call(
        section_kernel,
        grid_spec=pltpu.PrefetchScalarGridSpec(
            num_scalar_prefetch=1,
            grid=(steps,),
            in_specs=[
                anywhere,
                anywhere,
                pl.BlockSpec((1, model), lambda k, pad: (0, 0)),
                pl.BlockSpec((1, depth, 2, width), lambda k, pad: (0, k, 0, 0)),
            ],
            out_specs=[pl.BlockSpec(slab, lambda k, pad: (0, 0))] * 4,
            scratch_shapes=[
                pltpu.VMEM((steps, rows, depth), jnp.bfloat16),
                pltpu.VMEM((rows, model), jnp.bfloat16),
                pltpu.VMEM((rows, width), jnp.float32),
                pltpu.SemaphoreType.DMA((rows // 128,)),
            ],
        ),
        out_shape=[jax.ShapeDtypeStruct(slab, jnp.bfloat16)] * 4,
        cost_estimate=LIGHT,
        compiler_params=pltpu.CompilerParams(vmem_limit_bytes=VMEM),
    )(pad_counts, memory, targets, gains, weights)


def second_half_kernel(start_ref, w_ref, *out_refs):
    depth, width = w_ref.shape[1], w_ref.shape[3]
    found = w_ref[0].reshape(depth, 2 * width)[:, width:]
    for j, ref in enumerate(out_refs):
        size = ref.shape[0]
        ref[...] = found[j * size : (j + 1) * size]


def second_half(weights, start, depth, steps, pieces):
    width = weights.shape[3]
    return pl.pallas_call(
        second_half_kernel,
        grid_spec=pltpu.PrefetchScalarGridSpec(
            num_scalar_prefetch=1,
            grid=(steps,),
            in_specs=[pl.BlockSpec((1, depth, 2, width), lambda k, start: (0, start[0] + k, 0, 0))],
            out_specs=[pl.BlockSpec((depth // pieces, width), lambda k, start: (k, 0))] * pieces,
        ),
        out_shape=[jax.ShapeDtypeStruct((steps * depth // pieces, width), jnp.bfloat16)] * pieces,
        cost_estimate=LIGHT,
        compiler_params=pltpu.CompilerParams(vmem_limit_bytes=VMEM),
    )(start.reshape(1), weights)


def attend_kernel(first, half, chunks, *refs):
    if first:
        *slabs, acc_ref, peak_ref, total_ref, queries, keys, values, marks = refs
    else:
        *slabs, acc_ref, peak_ref, total_ref, out_a, out_b, queries, keys, values, marks = refs
    q_slabs, blocks = slabs[:4], slabs[4:]
    size = (blocks[0].shape[1] - MARK_ROWS) // 2
    z = position()[2]
    pieces = [ref.at[n] for ref in blocks for n in range(ref.shape[0])]
    for j, ref in enumerate(pieces):
        keys[j * size : (j + 1) * size, :] = ref[:size, :]
        values[j * size : (j + 1) * size, :] = ref[size : 2 * size, :]
        marks[:, j * size : (j + 1) * size] = ref[2 * size : 2 * size + 8, :].astype(jnp.float32)

    def run(at):
        base = at * 2 * half

        def take(index, when, top):
            @pl.when(when)
            def _():
                queries[pl.ds(top, half), :] = q_slabs[index][at * half : (at + 1) * half, :]

        take(2, z < 2, 0)
        take(0, z >= 2, 0)
        inner = (z == 1) | (z == 2)
        take(3, inner, half)
        take(1, jnp.logical_not(inner), half)

        part = 256
        for top in range(0, 2 * half, part):
            scores = lax.dot_general(
                queries[top : top + part, :],
                keys[...],
                (((1,), (1,)), ((), ())),
                preferred_element_type=jnp.float32,
            )
            scores = scores + marks[0:1, :]
            peak = jnp.max(scores, axis=1, keepdims=True)
            mine = slice(base + top, base + top + part)
            if not first:
                before = peak_ref[mine, :1]
                peak = jnp.maximum(peak, before)
                scale = jnp.exp(before - peak)
            soft = jnp.exp(scores - peak)
            total = jnp.sum(soft, axis=1, keepdims=True)
            mixed = jnp.dot(
                soft.astype(jnp.bfloat16), values[...], preferred_element_type=jnp.float32
            )
            if first:
                acc_ref[mine, :] = mixed
                peak_ref[mine, :] = jnp.broadcast_to(peak, (part, 128))
                total_ref[mine, :] = jnp.broadcast_to(total, (part, 128))
            else:
                mixed = mixed + scale * acc_ref[mine, :]
                total = total + scale * total_ref[mine, :1]
                found = (mixed / total).astype(jnp.bfloat16)
                if top < half:
                    out_a[at * half + top : at * half + top + part, :] = found
                else:
                    out_b[at * half + top - half : at * half + top - half + part, :] = found

    for at in range(chunks):
        run(at)


def attend(q_slabs, blocks, chunks, state=None):
    rows, dim = q_slabs[0].shape[0] - MARK_ROWS, q_slabs[0].shape[1]
    half = rows // chunks
    first = state is None
    keys = sum(b.shape[0] for b in blocks) * (blocks[0].shape[1] - MARK_ROWS) // 2
    vmem = pl.BlockSpec(memory_space=pltpu.VMEM)
    if first:
        out_shape = [jax.ShapeDtypeStruct((2 * rows, last), jnp.float32) for last in (dim, 128, 128)]
    else:
        out_shape = [jax.ShapeDtypeStruct((rows, dim), jnp.bfloat16)] * 2
    operands = [*q_slabs, *blocks, *(() if first else state)]
    return pl.pallas_call(
        functools.partial(attend_kernel, first, half, chunks),
        in_specs=[vmem] * len(operands),
        out_specs=[vmem] * len(out_shape),
        scratch_shapes=[
            pltpu.VMEM((2 * half, dim), jnp.bfloat16),
            pltpu.VMEM((keys, dim), jnp.bfloat16),
            pltpu.VMEM((keys, dim), jnp.bfloat16),
            pltpu.VMEM((8, keys), jnp.float32),
        ],
        out_shape=out_shape,
        cost_estimate=LIGHT,
        compiler_params=pltpu.CompilerParams(vmem_limit_bytes=ATTEND_VMEM),
    )(*operands)


def assemble_kernel(*refs):
    sources, mine, held, arrived = refs[:4], refs[4], refs[5], refs[6]
    x, y, z, core = position()
    odd = y % 2
    count, width = held.shape[:2]
    part = width // 2

    def fetch(j, action):
        wanted = (x + j) % count
        slot, arrival = held.at[j], arrived.at[j]

        @pl.when(z >= 2)
        def _():
            top = pl.multiple_of(wanted * width, width)
            action(pltpu.make_async_copy(mine.at[pl.ds(top, width)], slot, arrival))

        for n in range(2):

            @pl.when((z < 2) & ((wanted // 2 + z) % 2 == n))
            def _(n=n):
                for source, side in ((sources[n], core), (sources[2 + n], 1 - core)):
                    top = pl.multiple_of(side * part, part)
                    block = source.at[(wanted + odd) % 2]
                    action(pltpu.make_async_copy(block, slot.at[pl.ds(top, part)], arrival))

    for j in range(count):
        fetch(j, lambda copy: copy.start())
    for j in range(count):
        fetch(j, lambda copy: copy.wait())


def assemble(sources):
    count, (features, width) = 4, sources[4].shape
    shape = (count, features // count, width)
    return pl.pallas_call(
        assemble_kernel,
        in_specs=[pl.BlockSpec(memory_space=pl.ANY)] * 5,
        out_specs=pl.BlockSpec(memory_space=pltpu.VMEM),
        out_shape=jax.ShapeDtypeStruct(shape, jnp.bfloat16),
        scratch_shapes=[pltpu.SemaphoreType.DMA((count,))],
        cost_estimate=LIGHT,
        compiler_params=pltpu.CompilerParams(vmem_limit_bytes=SMALL_VMEM),
    )(*sources)


def project_kernel(distances, c0, c1, c2, c3, held, *refs):
    *out_refs, context = refs
    z = position()[2]
    dim = c0.shape[1]
    for d, ref in enumerate((c0, c1, c2, c3)):
        head = (z + 4 - d) % 4
        context[:, pl.ds(pl.multiple_of(head * dim, dim), dim)] = ref[...]
    parts = len(out_refs) // len(distances)
    for j, distance in enumerate(distances):
        mixed = lax.dot_general(
            context[...], held[distance], (((1,), (1,)), ((), ())), preferred_element_type=jnp.float32
        )
        for n, ref in enumerate(out_refs[j * parts : (j + 1) * parts]):
            size = ref.shape[0]
            ref[...] = mixed[n * size : (n + 1) * size].astype(ref.dtype)


def project(contexts, features, distances, dtype, parts=1):
    rows, dim = contexts[0].shape
    width = features.shape[1]
    outs = len(distances) * parts
    vmem = pl.BlockSpec(memory_space=pltpu.VMEM)
    return pl.pallas_call(
        functools.partial(project_kernel, distances),
        in_specs=[vmem] * 5,
        out_specs=[vmem] * outs,
        out_shape=[jax.ShapeDtypeStruct((rows // parts, width), dtype)] * outs,
        scratch_shapes=[pltpu.VMEM((rows, 4 * dim), jnp.bfloat16)],
        cost_estimate=LIGHT,
        compiler_params=pltpu.CompilerParams(vmem_limit_bytes=SMALL_VMEM),
    )(*contexts, features)


def joined_kernel(up_ref, down_ref, upward, downward, up_out, down_out):
    half = upward.shape[0]
    up_out[:half, :] = (up_ref[:half, :] + upward[...].astype(jnp.float32)).astype(jnp.bfloat16)
    up_out[half:, :] = up_ref[half:, :].astype(jnp.bfloat16)
    down_out[:half, :] = down_ref[:half, :].astype(jnp.bfloat16)
    down_out[half:, :] = (down_ref[half:, :] + downward[...].astype(jnp.float32)).astype(jnp.bfloat16)


def joined(up, down, upward, downward):
    vmem = pl.BlockSpec(memory_space=pltpu.VMEM)
    return pl.pallas_call(
        joined_kernel,
        in_specs=[vmem] * 4,
        out_specs=[vmem] * 2,
        out_shape=[jax.ShapeDtypeStruct(up.shape, jnp.bfloat16)] * 2,
        cost_estimate=LIGHT,
        compiler_params=pltpu.CompilerParams(vmem_limit_bytes=SMALL_VMEM),
    )(up, down, upward, downward)


def position():
    segment, ctx, x = (lax.axis_index(axis) for axis in AXES)
    core, y, low = ctx % 2, (ctx // 2) % 4, ctx // 8
    return x, y, 2 * segment + low, core


def after(value, *others):
    return lax.optimization_barrier((value, *others))[0]


def local(targets, memory, pad_counts, norm_gains, proj_weights):
    segment, ctx, x = (lax.axis_index(axis) for axis in AXES)
    core, y, low = ctx % 2, (ctx // 2) % 4, ctx // 8
    z = 2 * segment + low
    model, width = proj_weights.shape[1], proj_weights.shape[3]
    dim = width * 4 // HEADS
    rows = targets.shape[0]
    half = model // 2
    chunks = 2
    down = lambda x, y, z, c: (x, y, 3 - z, c)
    encoder = lambda x, y, z, c: z < 2
    decoder = lambda x, y, z, c: z >= 2
    flip = lambda x, y, z, c: (x, y, 1 - z, c)
    is_encoder = segment == 0

    odd = y % 2
    wanted_set = 2 * (1 - low) + odd
    (share,) = second_half(proj_weights, wanted_set * 2 + core, half // 8, 1, 1)
    p = moved(share, down, decoder)

    own, *to = section(after(pad_counts, share), memory, targets, norm_gains, proj_weights, dim)
    own, to, p = lax.optimization_barrier((own, to, p))
    beside = moved(p, lambda x, y, z, c: (x, y ^ 1, z, c), encoder)
    r1, r3, r2 = along_z(to[0], 1), along_z(to[2], 3), along_z(to[1], 2)
    early = jnp.where(is_encoder, own, jnp.where(z == 2, r1, r3))
    late = jnp.where(z == 0, r3, jnp.where(z == 1, r1, r2))
    pair = jnp.stack([early, late])
    pair, p, beside = lax.optimization_barrier((pair, p, beside))

    y1, y3 = along_y(pair, 1), along_y(pair, 3)
    lower = jnp.stack([p, beside])
    lower_twin = other_core(lower, encoder)
    upper = moved(lower, flip, encoder)
    (mine,) = second_half(after(proj_weights, pair), jnp.int32(2), half // 2, 2, 1)
    y1, y3, mine, lower_twin = lax.optimization_barrier((y1, y3, mine, lower_twin))

    far0, far1 = along_y(y1[0], 1), along_y(y3[1], 3)
    slabs = [own, r1, r2, r3]
    blocks = [pair, y1, y3]
    state = attend(slabs, blocks + [other_core(b) for b in blocks], chunks)
    far0, far1, *state = lax.optimization_barrier((far0, far1, *state))

    blocks = [far0[None], far1[None]]
    blocks = blocks + [other_core(b) for b in blocks]
    ca, cb = attend(slabs, blocks, chunks, state)
    upper_twin = other_core(after(upper, ca), encoder)
    contexts = [ca, along_z(cb, 1), along_z(ca, 2), along_z(cb, 3)]
    sources = [lower, upper, lower_twin, upper_twin, mine]
    out_width = model // 8
    residual = lax.dynamic_slice_in_dim(targets, (segment * 4 + x) * out_width, out_width, 1)
    features = assemble(sources)
    upward, downward = project(contexts, features, (2,), jnp.bfloat16, 2)
    contexts[0], upward, downward = lax.optimization_barrier((contexts[0], upward, downward))
    up, down = project(contexts, features, (1, 3), jnp.float32)
    up, down = joined(up, down, along_x(upward, 1), along_x(downward, 3))
    contexts[0], up, down = lax.optimization_barrier((contexts[0], up, down))
    (near,) = project(contexts, features, (0,), jnp.float32)
    summed = lax.optimization_barrier(residual.astype(jnp.float32) + near)
    for block, d in ((up, 1), (down, 3)):
        summed = summed + along_x(block, d).astype(jnp.float32)
    return summed.astype(jnp.bfloat16)


def solution(mesh):
    placed = (
        P("ctx", None),
        P("ctx", None),
        P("ctx"),
        P("segment", None),
        P("segment", None, None, "mp"),
    )
    return jax.shard_map(
        local, mesh=mesh, in_specs=placed, out_specs=P("ctx", ("segment", "mp")), check_vma=False
    )
```

```python
import functools

import jax
import jax.numpy as jnp
from jax import lax
from jax.experimental import pallas as pl
from jax.experimental.pallas import tpu as pltpu
from jax.sharding import PartitionSpec as P

HEADS = 16
AXES = ("segment", "ctx", "mp")
MARK_ROWS = 16
DEAD = -1e30
VMEM = 56 * 2**20
ATTEND_VMEM = 40 * 2**20
SMALL_VMEM = 24 * 2**20
LIGHT = pl.CostEstimate(flops=0, bytes_accessed=1024, transcendentals=0)


def device_of(x, y, z, core):
    return (z // 2) * 64 + (z % 2) * 32 + y * 8 + core * 4 + x


def place_of(i):
    return i % 4, (i // 8) % 4, (i // 64) * 2 + (i // 32) % 2, (i // 4) % 2


def moved(block, step, senders=lambda x, y, z, core: True):
    route = []
    for i in range(128):
        place = place_of(i)
        if senders(*place):
            x, y, z, core = step(*place)
            route.append((i, device_of(x % 4, y % 4, z % 4, core % 2)))
    return lax.ppermute(block, AXES, route)


def along_x(block, d):
    return moved(block, lambda x, y, z, c: (x + d, y, z, c))


def along_y(block, d, senders=lambda x, y, z, core: True):
    return moved(block, lambda x, y, z, c: (x, y + d, z, c), senders)


def along_z(block, d):
    return moved(block, lambda x, y, z, c: (x, y, z + d, c))


def other_core(block, senders=lambda x, y, z, core: True):
    return moved(block, lambda x, y, z, c: (x, y, z, c + 1), senders)


def norm_rows(hidden_rows, gain_row):
    widened = hidden_rows.astype(jnp.float32)
    inverse = lax.rsqrt(jnp.mean(widened * widened, axis=-1, keepdims=True) + 1e-06)
    return (widened * inverse * gain_row).astype(jnp.bfloat16)


def section_kernel(pad_ref, memory, targets, gain_ref, w_ref, *refs):
    *out_refs, normed, x_rows, total, arrival = refs
    k, steps = pl.program_id(0), pl.num_programs(0)
    depth, width = w_ref.shape[1], w_ref.shape[3]
    rows = total.shape[0]
    half = rows // 2
    dim = out_refs[0].shape[1]
    z = position()[2]
    encoder = z < 2

    def normalise(source, count):
        block = 128
        copies = [
            pltpu.make_async_copy(
                source.at[pl.ds(top, block)], x_rows.at[pl.ds(top, block)], arrival.at[top // block]
            )
            for top in range(0, count, block)
        ]
        for copy in copies:
            copy.start()
        for top in range(0, count, 64):
            if top % block == 0:
                copies[top // block].wait()
            part = norm_rows(x_rows[pl.ds(top, 64), :], gain_ref[...])
            for j in range(normed.shape[0]):
                normed[j, pl.ds(top, 64), :] = part[:, j * depth : (j + 1) * depth]

    @pl.when((k == 0) & encoder)
    def _():
        normalise(memory, half)

    @pl.when((k == 0) & jnp.logical_not(encoder))
    def _():
        normalise(targets, rows)

    def add(rows_of, found):
        @pl.when(k == 0)
        def _():
            total[rows_of, :] = found

        @pl.when(k > 0)
        def _():
            total[rows_of, :] += found

    @pl.when(encoder)
    def _():
        both = w_ref[0].reshape(depth, 2 * width)
        found = jnp.dot(normed[k, :half, :], both, preferred_element_type=jnp.float32)
        add(pl.ds(0, half), found[:, :width])
        add(pl.ds(half, half), found[:, width:])

    @pl.when(jnp.logical_not(encoder))
    def _():
        both = w_ref[0].reshape(depth, 2 * width)
        found = jnp.dot(normed[k], both[:, :width], preferred_element_type=jnp.float32)
        add(pl.ds(0, rows), found)

    @pl.when(k == steps - 1)
    def _():
        position = lax.broadcasted_iota(jnp.int32, (MARK_ROWS, dim), 1)
        marks = jnp.where(position < half - pad_ref[0], 0.0, DEAD).astype(jnp.bfloat16)
        for d, ref in enumerate(out_refs):
            head = (z + d) % 4
            ref[:rows, :] = total[:, pl.ds(pl.multiple_of(head * dim, dim), dim)].astype(jnp.bfloat16)
            ref[rows:, :] = marks


def section(pad_counts, memory, targets, gains, weights, dim):
    rows, model = targets.shape
    width = weights.shape[3]
    depth = 1024
    steps = model // depth
    slab = (rows + MARK_ROWS, dim)
    anywhere = pl.BlockSpec(memory_space=pl.ANY)
    return pl.pallas_call(
        section_kernel,
        grid_spec=pltpu.PrefetchScalarGridSpec(
            num_scalar_prefetch=1,
            grid=(steps,),
            in_specs=[
                anywhere,
                anywhere,
                pl.BlockSpec((1, model), lambda k, pad: (0, 0)),
                pl.BlockSpec((1, depth, 2, width), lambda k, pad: (0, k, 0, 0)),
            ],
            out_specs=[pl.BlockSpec(slab, lambda k, pad: (0, 0))] * 4,
            scratch_shapes=[
                pltpu.VMEM((steps, rows, depth), jnp.bfloat16),
                pltpu.VMEM((rows, model), jnp.bfloat16),
                pltpu.VMEM((rows, width), jnp.float32),
                pltpu.SemaphoreType.DMA((rows // 128,)),
            ],
        ),
        out_shape=[jax.ShapeDtypeStruct(slab, jnp.bfloat16)] * 4,
        cost_estimate=LIGHT,
        compiler_params=pltpu.CompilerParams(vmem_limit_bytes=VMEM),
    )(pad_counts, memory, targets, gains, weights)


def second_half_kernel(start_ref, w_ref, *out_refs):
    depth, width = w_ref.shape[1], w_ref.shape[3]
    found = w_ref[0].reshape(depth, 2 * width)[:, width:]
    for j, ref in enumerate(out_refs):
        size = ref.shape[0]
        ref[...] = found[j * size : (j + 1) * size]


def second_half(weights, start, depth, steps, pieces):
    width = weights.shape[3]
    return pl.pallas_call(
        second_half_kernel,
        grid_spec=pltpu.PrefetchScalarGridSpec(
            num_scalar_prefetch=1,
            grid=(steps,),
            in_specs=[pl.BlockSpec((1, depth, 2, width), lambda k, start: (0, start[0] + k, 0, 0))],
            out_specs=[pl.BlockSpec((depth // pieces, width), lambda k, start: (k, 0))] * pieces,
        ),
        out_shape=[jax.ShapeDtypeStruct((steps * depth // pieces, width), jnp.bfloat16)] * pieces,
        cost_estimate=LIGHT,
        compiler_params=pltpu.CompilerParams(vmem_limit_bytes=VMEM),
    )(start.reshape(1), weights)


def attend_kernel(first, half, chunks, *refs):
    if first:
        *slabs, acc_ref, peak_ref, total_ref, queries, keys, values, marks = refs
    else:
        *slabs, acc_ref, peak_ref, total_ref, out_a, out_b, queries, keys, values, marks = refs
    q_slabs, blocks = slabs[:4], slabs[4:]
    size = (blocks[0].shape[1] - MARK_ROWS) // 2
    z = position()[2]
    pieces = [ref.at[n] for ref in blocks for n in range(ref.shape[0])]
    for j, ref in enumerate(pieces):
        keys[j * size : (j + 1) * size, :] = ref[:size, :]
        values[j * size : (j + 1) * size, :] = ref[size : 2 * size, :]
        marks[:, j * size : (j + 1) * size] = ref[2 * size : 2 * size + 8, :].astype(jnp.float32)

    def run(at):
        base = at * 2 * half

        def take(index, when, top):
            @pl.when(when)
            def _():
                queries[pl.ds(top, half), :] = q_slabs[index][at * half : (at + 1) * half, :]

        take(2, z < 2, 0)
        take(0, z >= 2, 0)
        inner = (z == 1) | (z == 2)
        take(3, inner, half)
        take(1, jnp.logical_not(inner), half)

        part = 256
        for top in range(0, 2 * half, part):
            scores = lax.dot_general(
                queries[top : top + part, :],
                keys[...],
                (((1,), (1,)), ((), ())),
                preferred_element_type=jnp.float32,
            )
            scores = scores + marks[0:1, :]
            peak = jnp.max(scores, axis=1, keepdims=True)
            mine = slice(base + top, base + top + part)
            if not first:
                before = peak_ref[mine, :1]
                peak = jnp.maximum(peak, before)
                scale = jnp.exp(before - peak)
            soft = jnp.exp(scores - peak)
            total = jnp.sum(soft, axis=1, keepdims=True)
            mixed = jnp.dot(
                soft.astype(jnp.bfloat16), values[...], preferred_element_type=jnp.float32
            )
            if first:
                acc_ref[mine, :] = mixed
                peak_ref[mine, :] = jnp.broadcast_to(peak, (part, 128))
                total_ref[mine, :] = jnp.broadcast_to(total, (part, 128))
            else:
                mixed = mixed + scale * acc_ref[mine, :]
                total = total + scale * total_ref[mine, :1]
                found = (mixed / total).astype(jnp.bfloat16)
                if top < half:
                    out_a[at * half + top : at * half + top + part, :] = found
                else:
                    out_b[at * half + top - half : at * half + top - half + part, :] = found

    for at in range(chunks):
        run(at)


def attend(q_slabs, blocks, chunks, state=None):
    rows, dim = q_slabs[0].shape[0] - MARK_ROWS, q_slabs[0].shape[1]
    half = rows // chunks
    first = state is None
    keys = sum(b.shape[0] for b in blocks) * (blocks[0].shape[1] - MARK_ROWS) // 2
    vmem = pl.BlockSpec(memory_space=pltpu.VMEM)
    if first:
        out_shape = [jax.ShapeDtypeStruct((2 * rows, last), jnp.float32) for last in (dim, 128, 128)]
    else:
        out_shape = [jax.ShapeDtypeStruct((rows, dim), jnp.bfloat16)] * 2
    operands = [*q_slabs, *blocks, *(() if first else state)]
    return pl.pallas_call(
        functools.partial(attend_kernel, first, half, chunks),
        in_specs=[vmem] * len(operands),
        out_specs=[vmem] * len(out_shape),
        scratch_shapes=[
            pltpu.VMEM((2 * half, dim), jnp.bfloat16),
            pltpu.VMEM((keys, dim), jnp.bfloat16),
            pltpu.VMEM((keys, dim), jnp.bfloat16),
            pltpu.VMEM((8, keys), jnp.float32),
        ],
        out_shape=out_shape,
        cost_estimate=LIGHT,
        compiler_params=pltpu.CompilerParams(vmem_limit_bytes=ATTEND_VMEM),
    )(*operands)


def assemble_kernel(*refs):
    sources, mine, held, arrived = refs[:4], refs[4], refs[5], refs[6]
    x, y, z, core = position()
    odd = y % 2
    count, width = held.shape[:2]
    part = width // 2

    def fetch(j, action):
        wanted = (x + j) % count
        slot, arrival = held.at[j], arrived.at[j]

        @pl.when(z >= 2)
        def _():
            top = pl.multiple_of(wanted * width, width)
            action(pltpu.make_async_copy(mine.at[pl.ds(top, width)], slot, arrival))

        for n in range(2):

            @pl.when((z < 2) & ((wanted // 2 + z) % 2 == n))
            def _(n=n):
                for source, side in ((sources[n], core), (sources[2 + n], 1 - core)):
                    top = pl.multiple_of(side * part, part)
                    block = source.at[(wanted + odd) % 2]
                    action(pltpu.make_async_copy(block, slot.at[pl.ds(top, part)], arrival))

    for j in range(count):
        fetch(j, lambda copy: copy.start())
    for j in range(count):
        fetch(j, lambda copy: copy.wait())


def assemble(sources):
    count, (features, width) = 4, sources[4].shape
    shape = (count, features // count, width)
    return pl.pallas_call(
        assemble_kernel,
        in_specs=[pl.BlockSpec(memory_space=pl.ANY)] * 5,
        out_specs=pl.BlockSpec(memory_space=pltpu.VMEM),
        out_shape=jax.ShapeDtypeStruct(shape, jnp.bfloat16),
        scratch_shapes=[pltpu.SemaphoreType.DMA((count,))],
        cost_estimate=LIGHT,
        compiler_params=pltpu.CompilerParams(vmem_limit_bytes=SMALL_VMEM),
    )(*sources)


def project_kernel(distances, c0, c1, c2, c3, held, *refs):
    *out_refs, context = refs
    z = position()[2]
    dim = c0.shape[1]
    for d, ref in enumerate((c0, c1, c2, c3)):
        head = (z + 4 - d) % 4
        context[:, pl.ds(pl.multiple_of(head * dim, dim), dim)] = ref[...]
    parts = len(out_refs) // len(distances)
    for j, distance in enumerate(distances):
        mixed = lax.dot_general(
            context[...], held[distance], (((1,), (1,)), ((), ())), preferred_element_type=jnp.float32
        )
        for n, ref in enumerate(out_refs[j * parts : (j + 1) * parts]):
            size = ref.shape[0]
            ref[...] = mixed[n * size : (n + 1) * size].astype(ref.dtype)


def project(contexts, features, distances, dtype, parts=1):
    rows, dim = contexts[0].shape
    width = features.shape[1]
    outs = len(distances) * parts
    vmem = pl.BlockSpec(memory_space=pltpu.VMEM)
    return pl.pallas_call(
        functools.partial(project_kernel, distances),
        in_specs=[vmem] * 5,
        out_specs=[vmem] * outs,
        out_shape=[jax.ShapeDtypeStruct((rows // parts, width), dtype)] * outs,
        scratch_shapes=[pltpu.VMEM((rows, 4 * dim), jnp.bfloat16)],
        cost_estimate=LIGHT,
        compiler_params=pltpu.CompilerParams(vmem_limit_bytes=SMALL_VMEM),
    )(*contexts, features)


def joined_kernel(up_ref, down_ref, upward, downward, up_out, down_out):
    half = upward.shape[0]
    up_out[:half, :] = (up_ref[:half, :] + upward[...].astype(jnp.float32)).astype(jnp.bfloat16)
    up_out[half:, :] = up_ref[half:, :].astype(jnp.bfloat16)
    down_out[:half, :] = down_ref[:half, :].astype(jnp.bfloat16)
    down_out[half:, :] = (down_ref[half:, :] + downward[...].astype(jnp.float32)).astype(jnp.bfloat16)


def joined(up, down, upward, downward):
    vmem = pl.BlockSpec(memory_space=pltpu.VMEM)
    return pl.pallas_call(
        joined_kernel,
        in_specs=[vmem] * 4,
        out_specs=[vmem] * 2,
        out_shape=[jax.ShapeDtypeStruct(up.shape, jnp.bfloat16)] * 2,
        cost_estimate=LIGHT,
        compiler_params=pltpu.CompilerParams(vmem_limit_bytes=SMALL_VMEM),
    )(up, down, upward, downward)


def position():
    segment, ctx, x = (lax.axis_index(axis) for axis in AXES)
    core, y, low = ctx % 2, (ctx // 2) % 4, ctx // 8
    return x, y, 2 * segment + low, core


def after(value, *others):
    return lax.optimization_barrier((value, *others))[0]


def local(targets, memory, pad_counts, norm_gains, proj_weights):
    segment, ctx, x = (lax.axis_index(axis) for axis in AXES)
    core, y, low = ctx % 2, (ctx // 2) % 4, ctx // 8
    z = 2 * segment + low
    model, width = proj_weights.shape[1], proj_weights.shape[3]
    dim = width * 4 // HEADS
    rows = targets.shape[0]
    half = model // 2
    chunks = 2
    down = lambda x, y, z, c: (x, y, 3 - z, c)
    encoder = lambda x, y, z, c: z < 2
    decoder = lambda x, y, z, c: z >= 2
    flip = lambda x, y, z, c: (x, y, 1 - z, c)
    is_encoder = segment == 0

    odd = y % 2
    wanted_set = 2 * (1 - low) + odd
    (share,) = second_half(proj_weights, wanted_set * 2 + core, half // 8, 1, 1)
    p = moved(share, down, decoder)

    own, *to = section(after(pad_counts, share), memory, targets, norm_gains, proj_weights, dim)
    own, to, p = lax.optimization_barrier((own, to, p))
    beside = moved(p, lambda x, y, z, c: (x, y ^ 1, z, c), encoder)
    r1, r3, r2 = along_z(to[0], 1), along_z(to[2], 3), along_z(to[1], 2)
    early = jnp.where(is_encoder, own, jnp.where(z == 2, r1, r3))
    late = jnp.where(z == 0, r3, jnp.where(z == 1, r1, r2))
    pair = jnp.stack([early, late])
    pair, p = lax.optimization_barrier((pair, p))

    y1, y3 = along_y(pair, 1), along_y(pair, 3)
    lower = jnp.stack([p, beside])
    upper = moved(lower, flip, encoder)
    (mine,) = second_half(after(proj_weights, pair), jnp.int32(2), half // 2, 2, 1)
    y1, y3, mine = lax.optimization_barrier((y1, y3, mine))

    far0, far1 = along_y(y1[0], 1), along_y(y3[1], 3)
    slabs = [own, r1, r2, r3]
    blocks = [pair, y1, y3]
    state = attend(slabs, blocks + [other_core(b) for b in blocks], chunks)
    far0, far1, *state = lax.optimization_barrier((far0, far1, *state))

    blocks = [far0[None], far1[None]]
    blocks = blocks + [other_core(b) for b in blocks]
    ca, cb = attend(slabs, blocks, chunks, state)
    lower_twin = other_core(after(lower, state[0]), encoder)
    upper_twin = other_core(after(upper, ca), encoder)
    contexts = [ca, along_z(cb, 1), along_z(ca, 2), along_z(cb, 3)]
    sources = [lower, upper, lower_twin, upper_twin, mine]
    out_width = model // 8
    residual = lax.dynamic_slice_in_dim(targets, (segment * 4 + x) * out_width, out_width, 1)
    features = assemble(sources)
    upward, downward = project(contexts, features, (2,), jnp.bfloat16, 2)
    contexts[0], upward, downward = lax.optimization_barrier((contexts[0], upward, downward))
    up, down = project(contexts, features, (1, 3), jnp.float32)
    up, down = joined(up, down, along_x(upward, 1), along_x(downward, 3))
    contexts[0], up, down = lax.optimization_barrier((contexts[0], up, down))
    (near,) = project(contexts, features, (0,), jnp.float32)
    summed = lax.optimization_barrier(residual.astype(jnp.float32) + near)
    for block, d in ((up, 1), (down, 3)):
        summed = summed + along_x(block, d).astype(jnp.float32)
    return summed.astype(jnp.bfloat16)


def solution(mesh):
    placed = (
        P("ctx", None),
        P("ctx", None),
        P("ctx"),
        P("segment", None),
        P("segment", None, None, "mp"),
    )
    return jax.shard_map(
        local, mesh=mesh, in_specs=placed, out_specs=P("ctx", ("segment", "mp")), check_vma=False
    )
```

```python
import functools

import jax
import jax.numpy as jnp
from jax import lax
from jax.experimental import pallas as pl
from jax.experimental.pallas import tpu as pltpu
from jax.sharding import PartitionSpec as P

HEADS = 16
AXES = ("segment", "ctx", "mp")
MARK_ROWS = 16
DEAD = -1e30
VMEM = 56 * 2**20
ATTEND_VMEM = 40 * 2**20
SMALL_VMEM = 24 * 2**20
LIGHT = pl.CostEstimate(flops=0, bytes_accessed=1024, transcendentals=0)


def device_of(x, y, z, core):
    return (z // 2) * 64 + (z % 2) * 32 + y * 8 + core * 4 + x


def place_of(i):
    return i % 4, (i // 8) % 4, (i // 64) * 2 + (i // 32) % 2, (i // 4) % 2


def moved(block, step, senders=lambda x, y, z, core: True):
    route = []
    for i in range(128):
        place = place_of(i)
        if senders(*place):
            x, y, z, core = step(*place)
            route.append((i, device_of(x % 4, y % 4, z % 4, core % 2)))
    return lax.ppermute(block, AXES, route)


def along_x(block, d):
    return moved(block, lambda x, y, z, c: (x + d, y, z, c))


def along_y(block, d, senders=lambda x, y, z, core: True):
    return moved(block, lambda x, y, z, c: (x, y + d, z, c), senders)


def along_z(block, d):
    return moved(block, lambda x, y, z, c: (x, y, z + d, c))


def other_core(block, senders=lambda x, y, z, core: True):
    return moved(block, lambda x, y, z, c: (x, y, z, c + 1), senders)


def norm_rows(hidden_rows, gain_row):
    widened = hidden_rows.astype(jnp.float32)
    inverse = lax.rsqrt(jnp.mean(widened * widened, axis=-1, keepdims=True) + 1e-06)
    return (widened * inverse * gain_row).astype(jnp.bfloat16)


def section_kernel(pad_ref, memory, targets, gain_ref, w_ref, *refs):
    *out_refs, normed, x_rows, total, arrival = refs
    k, steps = pl.program_id(0), pl.num_programs(0)
    depth, width = w_ref.shape[1], w_ref.shape[3]
    rows = total.shape[0]
    half = rows // 2
    dim = out_refs[0].shape[1]
    z = position()[2]
    encoder = z < 2

    def normalise(source, count):
        block = 128
        copies = [
            pltpu.make_async_copy(
                source.at[pl.ds(top, block)], x_rows.at[pl.ds(top, block)], arrival.at[top // block]
            )
            for top in range(0, count, block)
        ]
        for copy in copies:
            copy.start()
        for top in range(0, count, 64):
            if top % block == 0:
                copies[top // block].wait()
            part = norm_rows(x_rows[pl.ds(top, 64), :], gain_ref[...])
            for j in range(normed.shape[0]):
                normed[j, pl.ds(top, 64), :] = part[:, j * depth : (j + 1) * depth]

    @pl.when((k == 0) & encoder)
    def _():
        normalise(memory, half)

    @pl.when((k == 0) & jnp.logical_not(encoder))
    def _():
        normalise(targets, rows)

    def add(rows_of, found):
        @pl.when(k == 0)
        def _():
            total[rows_of, :] = found

        @pl.when(k > 0)
        def _():
            total[rows_of, :] += found

    @pl.when(encoder)
    def _():
        both = w_ref[0].reshape(depth, 2 * width)
        found = jnp.dot(normed[k, :half, :], both, preferred_element_type=jnp.float32)
        add(pl.ds(0, half), found[:, :width])
        add(pl.ds(half, half), found[:, width:])

    @pl.when(jnp.logical_not(encoder))
    def _():
        both = w_ref[0].reshape(depth, 2 * width)
        found = jnp.dot(normed[k], both[:, :width], preferred_element_type=jnp.float32)
        add(pl.ds(0, rows), found)

    @pl.when(k == steps - 1)
    def _():
        position = lax.broadcasted_iota(jnp.int32, (MARK_ROWS, dim), 1)
        marks = jnp.where(position < half - pad_ref[0], 0.0, DEAD).astype(jnp.bfloat16)
        for d, ref in enumerate(out_refs):
            head = (z + d) % 4
            ref[:rows, :] = total[:, pl.ds(pl.multiple_of(head * dim, dim), dim)].astype(jnp.bfloat16)
            ref[rows:, :] = marks


def section(pad_counts, memory, targets, gains, weights, dim):
    rows, model = targets.shape
    width = weights.shape[3]
    depth = 1024
    steps = model // depth
    slab = (rows + MARK_ROWS, dim)
    anywhere = pl.BlockSpec(memory_space=pl.ANY)
    return pl.pallas_call(
        section_kernel,
        grid_spec=pltpu.PrefetchScalarGridSpec(
            num_scalar_prefetch=1,
            grid=(steps,),
            in_specs=[
                anywhere,
                anywhere,
                pl.BlockSpec((1, model), lambda k, pad: (0, 0)),
                pl.BlockSpec((1, depth, 2, width), lambda k, pad: (0, k, 0, 0)),
            ],
            out_specs=[pl.BlockSpec(slab, lambda k, pad: (0, 0))] * 4,
            scratch_shapes=[
                pltpu.VMEM((steps, rows, depth), jnp.bfloat16),
                pltpu.VMEM((rows, model), jnp.bfloat16),
                pltpu.VMEM((rows, width), jnp.float32),
                pltpu.SemaphoreType.DMA((rows // 128,)),
            ],
        ),
        out_shape=[jax.ShapeDtypeStruct(slab, jnp.bfloat16)] * 4,
        cost_estimate=LIGHT,
        compiler_params=pltpu.CompilerParams(vmem_limit_bytes=VMEM),
    )(pad_counts, memory, targets, gains, weights)


def second_half_kernel(start_ref, w_ref, *out_refs):
    depth, width = w_ref.shape[1], w_ref.shape[3]
    found = w_ref[0].reshape(depth, 2 * width)[:, width:]
    for j, ref in enumerate(out_refs):
        size = ref.shape[0]
        ref[...] = found[j * size : (j + 1) * size]


def second_half(weights, start, depth, steps, pieces):
    width = weights.shape[3]
    return pl.pallas_call(
        second_half_kernel,
        grid_spec=pltpu.PrefetchScalarGridSpec(
            num_scalar_prefetch=1,
            grid=(steps,),
            in_specs=[pl.BlockSpec((1, depth, 2, width), lambda k, start: (0, start[0] + k, 0, 0))],
            out_specs=[pl.BlockSpec((depth // pieces, width), lambda k, start: (k, 0))] * pieces,
        ),
        out_shape=[jax.ShapeDtypeStruct((steps * depth // pieces, width), jnp.bfloat16)] * pieces,
        cost_estimate=LIGHT,
        compiler_params=pltpu.CompilerParams(vmem_limit_bytes=VMEM),
    )(start.reshape(1), weights)


def share_kernel(w_ref, out_ref, held, arrived):
    x, y, z, core = position()
    size, width = out_ref.shape
    index = (2 * (1 - z % 2) + y % 2) * 2 + core
    top = pl.multiple_of(index * size, size)
    copy = pltpu.make_async_copy(w_ref.at[0, pl.ds(top, size)], held, arrived)
    copy.start()
    copy.wait()
    out_ref[...] = held[...].reshape(size, 2 * width)[:, width:]


def share_of(weights, size):
    width = weights.shape[3]
    return pl.pallas_call(
        share_kernel,
        in_specs=[pl.BlockSpec(memory_space=pl.ANY)],
        out_specs=pl.BlockSpec(memory_space=pltpu.VMEM),
        out_shape=jax.ShapeDtypeStruct((size, width), jnp.bfloat16),
        scratch_shapes=[pltpu.VMEM((size, 2, width), jnp.bfloat16), pltpu.SemaphoreType.DMA],
        cost_estimate=LIGHT,
        compiler_params=pltpu.CompilerParams(vmem_limit_bytes=VMEM),
    )(weights)


def attend_kernel(first, half, chunks, *refs):
    if first:
        *slabs, acc_ref, peak_ref, total_ref, queries, keys, values, marks = refs
    else:
        *slabs, acc_ref, peak_ref, total_ref, out_a, out_b, queries, keys, values, marks = refs
    q_slabs, blocks = slabs[:4], slabs[4:]
    size = (blocks[0].shape[1] - MARK_ROWS) // 2
    z = position()[2]
    pieces = [ref.at[n] for ref in blocks for n in range(ref.shape[0])]
    for j, ref in enumerate(pieces):
        keys[j * size : (j + 1) * size, :] = ref[:size, :]
        values[j * size : (j + 1) * size, :] = ref[size : 2 * size, :]
        marks[:, j * size : (j + 1) * size] = ref[2 * size : 2 * size + 8, :].astype(jnp.float32)

    def run(at):
        base = at * 2 * half

        def take(index, when, top):
            @pl.when(when)
            def _():
                queries[pl.ds(top, half), :] = q_slabs[index][at * half : (at + 1) * half, :]

        take(2, z < 2, 0)
        take(0, z >= 2, 0)
        inner = (z == 1) | (z == 2)
        take(3, inner, half)
        take(1, jnp.logical_not(inner), half)

        part = 256
        for top in range(0, 2 * half, part):
            scores = lax.dot_general(
                queries[top : top + part, :],
                keys[...],
                (((1,), (1,)), ((), ())),
                preferred_element_type=jnp.float32,
            )
            scores = scores + marks[0:1, :]
            peak = jnp.max(scores, axis=1, keepdims=True)
            mine = slice(base + top, base + top + part)
            if not first:
                before = peak_ref[mine, :1]
                peak = jnp.maximum(peak, before)
                scale = jnp.exp(before - peak)
            soft = jnp.exp(scores - peak)
            total = jnp.sum(soft, axis=1, keepdims=True)
            mixed = jnp.dot(
                soft.astype(jnp.bfloat16), values[...], preferred_element_type=jnp.float32
            )
            if first:
                acc_ref[mine, :] = mixed
                peak_ref[mine, :] = jnp.broadcast_to(peak, (part, 128))
                total_ref[mine, :] = jnp.broadcast_to(total, (part, 128))
            else:
                mixed = mixed + scale * acc_ref[mine, :]
                total = total + scale * total_ref[mine, :1]
                found = (mixed / total).astype(jnp.bfloat16)
                if top < half:
                    out_a[at * half + top : at * half + top + part, :] = found
                else:
                    out_b[at * half + top - half : at * half + top - half + part, :] = found

    for at in range(chunks):
        run(at)


def attend(q_slabs, blocks, chunks, state=None):
    rows, dim = q_slabs[0].shape[0] - MARK_ROWS, q_slabs[0].shape[1]
    half = rows // chunks
    first = state is None
    keys = sum(b.shape[0] for b in blocks) * (blocks[0].shape[1] - MARK_ROWS) // 2
    vmem = pl.BlockSpec(memory_space=pltpu.VMEM)
    if first:
        out_shape = [jax.ShapeDtypeStruct((2 * rows, last), jnp.float32) for last in (dim, 128, 128)]
    else:
        out_shape = [jax.ShapeDtypeStruct((rows, dim), jnp.bfloat16)] * 2
    operands = [*q_slabs, *blocks, *(() if first else state)]
    return pl.pallas_call(
        functools.partial(attend_kernel, first, half, chunks),
        in_specs=[vmem] * len(operands),
        out_specs=[vmem] * len(out_shape),
        scratch_shapes=[
            pltpu.VMEM((2 * half, dim), jnp.bfloat16),
            pltpu.VMEM((keys, dim), jnp.bfloat16),
            pltpu.VMEM((keys, dim), jnp.bfloat16),
            pltpu.VMEM((8, keys), jnp.float32),
        ],
        out_shape=out_shape,
        cost_estimate=LIGHT,
        compiler_params=pltpu.CompilerParams(vmem_limit_bytes=ATTEND_VMEM),
    )(*operands)


def assemble_kernel(*refs):
    sources, mine, held, arrived = refs[:4], refs[4], refs[5], refs[6]
    x, y, z, core = position()
    odd = y % 2
    count, width = held.shape[:2]
    part = width // 2

    def fetch(j, action):
        wanted = (x + j) % count
        slot, arrival = held.at[j], arrived.at[j]

        @pl.when(z >= 2)
        def _():
            top = pl.multiple_of(wanted * width, width)
            action(pltpu.make_async_copy(mine.at[pl.ds(top, width)], slot, arrival))

        for n in range(2):

            @pl.when((z < 2) & ((wanted // 2 + z) % 2 == n))
            def _(n=n):
                for source, side in ((sources[n], core), (sources[2 + n], 1 - core)):
                    top = pl.multiple_of(side * part, part)
                    block = source.at[(wanted + odd) % 2]
                    action(pltpu.make_async_copy(block, slot.at[pl.ds(top, part)], arrival))

    for j in range(count):
        fetch(j, lambda copy: copy.start())
    for j in range(count):
        fetch(j, lambda copy: copy.wait())


def assemble(sources):
    count, (features, width) = 4, sources[4].shape
    shape = (count, features // count, width)
    return pl.pallas_call(
        assemble_kernel,
        in_specs=[pl.BlockSpec(memory_space=pl.ANY)] * 5,
        out_specs=pl.BlockSpec(memory_space=pltpu.VMEM),
        out_shape=jax.ShapeDtypeStruct(shape, jnp.bfloat16),
        scratch_shapes=[pltpu.SemaphoreType.DMA((count,))],
        cost_estimate=LIGHT,
        compiler_params=pltpu.CompilerParams(vmem_limit_bytes=SMALL_VMEM),
    )(*sources)


def project_kernel(distances, c0, c1, c2, c3, held, *refs):
    *out_refs, context = refs
    z = position()[2]
    dim = c0.shape[1]
    for d, ref in enumerate((c0, c1, c2, c3)):
        head = (z + 4 - d) % 4
        context[:, pl.ds(pl.multiple_of(head * dim, dim), dim)] = ref[...]
    parts = len(out_refs) // len(distances)
    for j, distance in enumerate(distances):
        mixed = lax.dot_general(
            context[...], held[distance], (((1,), (1,)), ((), ())), preferred_element_type=jnp.float32
        )
        for n, ref in enumerate(out_refs[j * parts : (j + 1) * parts]):
            size = ref.shape[0]
            ref[...] = mixed[n * size : (n + 1) * size].astype(ref.dtype)


def project(contexts, features, distances, dtypes):
    rows, dim = contexts[0].shape
    width = features.shape[1]
    outs = len(dtypes)
    parts = outs // len(distances)
    vmem = pl.BlockSpec(memory_space=pltpu.VMEM)
    return pl.pallas_call(
        functools.partial(project_kernel, distances),
        in_specs=[vmem] * 5,
        out_specs=[vmem] * outs,
        out_shape=[jax.ShapeDtypeStruct((rows // parts, width), dtype) for dtype in dtypes],
        scratch_shapes=[pltpu.VMEM((rows, 4 * dim), jnp.bfloat16)],
        cost_estimate=LIGHT,
        compiler_params=pltpu.CompilerParams(vmem_limit_bytes=SMALL_VMEM),
    )(*contexts, features)


def joined_kernel(up_ref, down_ref, upward, downward, up_out, down_out):
    up_out[...] = (up_ref[...] + upward[...].astype(jnp.float32)).astype(jnp.bfloat16)
    down_out[...] = (down_ref[...] + downward[...].astype(jnp.float32)).astype(jnp.bfloat16)


def joined(*operands):
    vmem = pl.BlockSpec(memory_space=pltpu.VMEM)
    return pl.pallas_call(
        joined_kernel,
        in_specs=[vmem] * 4,
        out_specs=[vmem] * 2,
        out_shape=[jax.ShapeDtypeStruct(operands[2].shape, jnp.bfloat16)] * 2,
        cost_estimate=LIGHT,
        compiler_params=pltpu.CompilerParams(vmem_limit_bytes=SMALL_VMEM),
    )(*operands)


def finish_kernel(residual, near_top, near_end, up_top, up_end, down_top, down_end, out_ref):
    half = up_top.shape[0]
    for top, near, one, other in ((0, near_top, up_top, down_top), (half, near_end, up_end, down_end)):
        rows = slice(top, top + half)
        found = residual[rows, :].astype(jnp.float32) + near[...]
        found = found + one[...].astype(jnp.float32) + other[...].astype(jnp.float32)
        out_ref[rows, :] = found.astype(jnp.bfloat16)


def finish(residual, *parts):
    vmem = pl.BlockSpec(memory_space=pltpu.VMEM)
    return pl.pallas_call(
        finish_kernel,
        in_specs=[vmem] * 7,
        out_specs=vmem,
        out_shape=jax.ShapeDtypeStruct(residual.shape, jnp.bfloat16),
        cost_estimate=LIGHT,
        compiler_params=pltpu.CompilerParams(vmem_limit_bytes=SMALL_VMEM),
    )(residual, *parts)


def position():
    segment, ctx, x = (lax.axis_index(axis) for axis in AXES)
    core, y, low = ctx % 2, (ctx // 2) % 4, ctx // 8
    return x, y, 2 * segment + low, core


def after(value, *others):
    return lax.optimization_barrier((value, *others))[0]


def local(targets, memory, pad_counts, norm_gains, proj_weights):
    segment, ctx, x = (lax.axis_index(axis) for axis in AXES)
    core, y, low = ctx % 2, (ctx // 2) % 4, ctx // 8
    z = 2 * segment + low
    model, width = proj_weights.shape[1], proj_weights.shape[3]
    dim = width * 4 // HEADS
    rows = targets.shape[0]
    half = model // 2
    chunks = 2
    down = lambda x, y, z, c: (x, y, 3 - z, c)
    encoder = lambda x, y, z, c: z < 2
    decoder = lambda x, y, z, c: z >= 2
    flip = lambda x, y, z, c: (x, y, 1 - z, c)
    is_encoder = segment == 0

    share = share_of(proj_weights, half // 8)
    p = moved(share, down, decoder)

    own, *to = section(after(pad_counts, share), memory, targets, norm_gains, proj_weights, dim)
    own, to, p = lax.optimization_barrier((own, to, p))
    beside = moved(p, lambda x, y, z, c: (x, y ^ 1, z, c), encoder)
    r1, r3, r2 = along_z(to[0], 1), along_z(to[2], 3), along_z(to[1], 2)
    early = jnp.where(is_encoder, own, jnp.where(z == 2, r1, r3))
    late = jnp.where(z == 0, r3, jnp.where(z == 1, r1, r2))
    pair = jnp.stack([early, late])
    pair, p = lax.optimization_barrier((pair, p))

    y1, y3 = along_y(pair, 1), along_y(pair, 3)
    lower = jnp.stack([p, beside])
    upper = moved(lower, flip, encoder)
    (mine,) = second_half(after(proj_weights, pair), jnp.int32(2), half // 2, 2, 1)
    y1, y3, mine = lax.optimization_barrier((y1, y3, mine))

    far0, far1 = along_y(y1[0], 1), along_y(y3[1], 3)
    slabs = [own, r1, r2, r3]
    blocks = [pair, y1, y3]
    state = attend(slabs, blocks + [other_core(b) for b in blocks], chunks)
    far0, far1, *state = lax.optimization_barrier((far0, far1, *state))

    blocks = [far0[None], far1[None]]
    blocks = blocks + [other_core(b) for b in blocks]
    ca, cb = attend(slabs, blocks, chunks, state)
    lower_twin = other_core(after(lower, state[0]), encoder)
    upper_twin = other_core(after(upper, ca), encoder)
    contexts = [ca, along_z(cb, 1), along_z(ca, 2), along_z(cb, 3)]
    sources = [lower, upper, lower_twin, upper_twin, mine]
    out_width = model // 8
    residual = lax.dynamic_slice_in_dim(targets, (segment * 4 + x) * out_width, out_width, 1)
    features = assemble(sources)
    wide, narrow = jnp.float32, jnp.bfloat16
    wide, narrow = jnp.float32, jnp.bfloat16
    upward, downward = project(contexts, features, (2,), (narrow, narrow))
    contexts[0], upward, downward = lax.optimization_barrier((contexts[0], upward, downward))
    up_top, up_end, down_top, down_end, near_top, near_end = project(
        contexts, features, (1, 3, 0), (wide, narrow, narrow, wide, wide, wide)
    )
    up_end, down_top = along_x(up_end, 1), along_x(down_top, 3)
    up_top, down_end = joined(up_top, down_end, along_x(upward, 1), along_x(downward, 3))
    up_top, down_end = along_x(up_top, 1), along_x(down_end, 3)
    return finish(residual, near_top, near_end, up_top, up_end, down_top, down_end)


def solution(mesh):
    placed = (
        P("ctx", None),
        P("ctx", None),
        P("ctx"),
        P("segment", None),
        P("segment", None, None, "mp"),
    )
    return jax.shard_map(
        local, mesh=mesh, in_specs=placed, out_specs=P("ctx", ("segment", "mp")), check_vma=False
    )
```

```python
import functools

import jax
import jax.numpy as jnp
from jax import lax
from jax.experimental import pallas as pl
from jax.experimental.pallas import tpu as pltpu
from jax.sharding import PartitionSpec as P

HEADS = 16
AXES = ("segment", "ctx", "mp")
MARK_ROWS = 16
DEAD = -1e30
VMEM = 56 * 2**20
ATTEND_VMEM = 40 * 2**20
SMALL_VMEM = 24 * 2**20
LIGHT = pl.CostEstimate(flops=0, bytes_accessed=1024, transcendentals=0)


def device_of(x, y, z, core):
    return (z // 2) * 64 + (z % 2) * 32 + y * 8 + core * 4 + x


def place_of(i):
    return i % 4, (i // 8) % 4, (i // 64) * 2 + (i // 32) % 2, (i // 4) % 2


def moved(block, step, senders=lambda x, y, z, core: True):
    route = []
    for i in range(128):
        place = place_of(i)
        if senders(*place):
            x, y, z, core = step(*place)
            route.append((i, device_of(x % 4, y % 4, z % 4, core % 2)))
    return lax.ppermute(block, AXES, route)


def along_x(block, d):
    return moved(block, lambda x, y, z, c: (x + d, y, z, c))


def along_y(block, d, senders=lambda x, y, z, core: True):
    return moved(block, lambda x, y, z, c: (x, y + d, z, c), senders)


def along_z(block, d):
    return moved(block, lambda x, y, z, c: (x, y, z + d, c))


def other_core(block, senders=lambda x, y, z, core: True):
    return moved(block, lambda x, y, z, c: (x, y, z, c + 1), senders)


def norm_rows(hidden_rows, gain_row):
    widened = hidden_rows.astype(jnp.float32)
    inverse = lax.rsqrt(jnp.mean(widened * widened, axis=-1, keepdims=True) + 1e-06)
    return (widened * inverse * gain_row).astype(jnp.bfloat16)


def section_kernel(pad_ref, memory, targets, gain_ref, weights, *refs):
    *out_refs, normed, x_rows, total, blocks, arrival, block_arrival = refs
    steps, depth, _, width = blocks.shape
    rows = total.shape[0]
    half = rows // 2
    dim = out_refs[0].shape[1]
    z = position()[2]
    encoder = z < 2

    def block_copy(k):
        source = weights.at[0, pl.ds(pl.multiple_of(k * depth, depth), depth)]
        return pltpu.make_async_copy(source, blocks.at[k], block_arrival.at[k])

    def normalise(source, count):
        block = 128
        copies = [
            pltpu.make_async_copy(
                source.at[pl.ds(top, block)], x_rows.at[pl.ds(top, block)], arrival.at[top // block]
            )
            for top in range(0, count, block)
        ]
        for copy in copies:
            copy.start()
        for k in range(steps // 2):
            block_copy(k).start()
        for top in range(0, count, 64):
            if top % block == 0:
                copies[top // block].wait()
            part = norm_rows(x_rows[pl.ds(top, 64), :], gain_ref[...])
            for j in range(normed.shape[0]):
                normed[j, pl.ds(top, 64), :] = part[:, j * depth : (j + 1) * depth]

    @pl.when(encoder)
    def _():
        normalise(memory, half)

    @pl.when(jnp.logical_not(encoder))
    def _():
        normalise(targets, rows)

    for k in range(steps // 2, steps):
        block_copy(k).start()
    total[...] = jnp.zeros_like(total)

    @pl.loop(0, steps)
    def _(k):
        block_copy(k).wait()

        @pl.when(encoder)
        def _():
            both = blocks[k].reshape(depth, 2 * width)
            found = jnp.dot(normed[k, :half, :], both, preferred_element_type=jnp.float32)
            total[:half, :] += found[:, :width]
            total[half:, :] += found[:, width:]

        @pl.when(jnp.logical_not(encoder))
        def _():
            both = blocks[k].reshape(depth, 2 * width)
            total[...] += jnp.dot(normed[k], both[:, :width], preferred_element_type=jnp.float32)

    columns = lax.broadcasted_iota(jnp.int32, (MARK_ROWS, dim), 1)
    marks = jnp.where(columns < half - pad_ref[0], 0.0, DEAD).astype(jnp.bfloat16)
    for d, ref in enumerate(out_refs):
        head = (z + d) % 4
        ref[:rows, :] = total[:, pl.ds(pl.multiple_of(head * dim, dim), dim)].astype(jnp.bfloat16)
        ref[rows:, :] = marks


def section(pad_counts, memory, targets, gains, weights, dim):
    rows, model = targets.shape
    width = weights.shape[3]
    depth = 1024
    steps = model // depth
    slab = (rows + MARK_ROWS, dim)
    anywhere = pl.BlockSpec(memory_space=pl.ANY)
    vmem = pl.BlockSpec(memory_space=pltpu.VMEM)
    return pl.pallas_call(
        section_kernel,
        in_specs=[pl.BlockSpec(memory_space=pltpu.SMEM), anywhere, anywhere, vmem, anywhere],
        out_specs=[vmem] * 4,
        scratch_shapes=[
            pltpu.VMEM((steps, rows, depth), jnp.bfloat16),
            pltpu.VMEM((rows, model), jnp.bfloat16),
            pltpu.VMEM((rows, width), jnp.float32),
            pltpu.VMEM((steps, depth, 2, width), jnp.bfloat16),
            pltpu.SemaphoreType.DMA((rows // 128,)),
            pltpu.SemaphoreType.DMA((steps,)),
        ],
        out_shape=[jax.ShapeDtypeStruct(slab, jnp.bfloat16)] * 4,
        cost_estimate=LIGHT,
        compiler_params=pltpu.CompilerParams(vmem_limit_bytes=VMEM),
    )(pad_counts, memory, targets, gains, weights)


def second_half_kernel(start_ref, w_ref, *out_refs):
    depth, width = w_ref.shape[1], w_ref.shape[3]
    found = w_ref[0].reshape(depth, 2 * width)[:, width:]
    for j, ref in enumerate(out_refs):
        size = ref.shape[0]
        ref[...] = found[j * size : (j + 1) * size]


def second_half(weights, start, depth, steps, pieces):
    width = weights.shape[3]
    return pl.pallas_call(
        second_half_kernel,
        grid_spec=pltpu.PrefetchScalarGridSpec(
            num_scalar_prefetch=1,
            grid=(steps,),
            in_specs=[pl.BlockSpec((1, depth, 2, width), lambda k, start: (0, start[0] + k, 0, 0))],
            out_specs=[pl.BlockSpec((depth // pieces, width), lambda k, start: (k, 0))] * pieces,
        ),
        out_shape=[jax.ShapeDtypeStruct((steps * depth // pieces, width), jnp.bfloat16)] * pieces,
        cost_estimate=LIGHT,
        compiler_params=pltpu.CompilerParams(vmem_limit_bytes=VMEM),
    )(start.reshape(1), weights)


def share_kernel(w_ref, out_ref, held, arrived):
    x, y, z, core = position()
    size, width = out_ref.shape
    index = (2 * (1 - z % 2) + y % 2) * 2 + core
    top = pl.multiple_of(index * size, size)
    copy = pltpu.make_async_copy(w_ref.at[0, pl.ds(top, size)], held, arrived)
    copy.start()
    copy.wait()
    out_ref[...] = held[...].reshape(size, 2 * width)[:, width:]


def share_of(weights, size):
    width = weights.shape[3]
    return pl.pallas_call(
        share_kernel,
        in_specs=[pl.BlockSpec(memory_space=pl.ANY)],
        out_specs=pl.BlockSpec(memory_space=pltpu.VMEM),
        out_shape=jax.ShapeDtypeStruct((size, width), jnp.bfloat16),
        scratch_shapes=[pltpu.VMEM((size, 2, width), jnp.bfloat16), pltpu.SemaphoreType.DMA],
        cost_estimate=LIGHT,
        compiler_params=pltpu.CompilerParams(vmem_limit_bytes=VMEM),
    )(weights)


def attend_kernel(first, half, chunks, *refs):
    if first:
        *slabs, acc_ref, peak_ref, total_ref, queries, keys, values, marks = refs
    else:
        *slabs, acc_ref, peak_ref, total_ref, out_a, out_b, queries, keys, values, marks = refs
    q_slabs, blocks = slabs[:4], slabs[4:]
    size = (blocks[0].shape[1] - MARK_ROWS) // 2
    z = position()[2]
    pieces = [ref.at[n] for ref in blocks for n in range(ref.shape[0])]
    for j, ref in enumerate(pieces):
        keys[j * size : (j + 1) * size, :] = ref[:size, :]
        values[j * size : (j + 1) * size, :] = ref[size : 2 * size, :]
        marks[:, j * size : (j + 1) * size] = ref[2 * size : 2 * size + 8, :].astype(jnp.float32)

    def run(at):
        base = at * 2 * half

        def take(index, when, top):
            @pl.when(when)
            def _():
                queries[pl.ds(top, half), :] = q_slabs[index][at * half : (at + 1) * half, :]

        take(2, z < 2, 0)
        take(0, z >= 2, 0)
        inner = (z == 1) | (z == 2)
        take(3, inner, half)
        take(1, jnp.logical_not(inner), half)

        part = 256
        for top in range(0, 2 * half, part):
            scores = lax.dot_general(
                queries[top : top + part, :],
                keys[...],
                (((1,), (1,)), ((), ())),
                preferred_element_type=jnp.float32,
            )
            scores = scores + marks[0:1, :]
            peak = jnp.max(scores, axis=1, keepdims=True)
            mine = slice(base + top, base + top + part)
            if not first:
                before = peak_ref[mine, :1]
                peak = jnp.maximum(peak, before)
                scale = jnp.exp(before - peak)
            soft = jnp.exp(scores - peak)
            total = jnp.sum(soft, axis=1, keepdims=True)
            mixed = jnp.dot(
                soft.astype(jnp.bfloat16), values[...], preferred_element_type=jnp.float32
            )
            if first:
                acc_ref[mine, :] = mixed
                peak_ref[mine, :] = jnp.broadcast_to(peak, (part, 128))
                total_ref[mine, :] = jnp.broadcast_to(total, (part, 128))
            else:
                mixed = mixed + scale * acc_ref[mine, :]
                total = total + scale * total_ref[mine, :1]
                found = (mixed / total).astype(jnp.bfloat16)
                if top < half:
                    out_a[at * half + top : at * half + top + part, :] = found
                else:
                    out_b[at * half + top - half : at * half + top - half + part, :] = found

    for at in range(chunks):
        run(at)


def attend(q_slabs, blocks, chunks, state=None):
    rows, dim = q_slabs[0].shape[0] - MARK_ROWS, q_slabs[0].shape[1]
    half = rows // chunks
    first = state is None
    keys = sum(b.shape[0] for b in blocks) * (blocks[0].shape[1] - MARK_ROWS) // 2
    vmem = pl.BlockSpec(memory_space=pltpu.VMEM)
    if first:
        out_shape = [jax.ShapeDtypeStruct((2 * rows, last), jnp.float32) for last in (dim, 128, 128)]
    else:
        out_shape = [jax.ShapeDtypeStruct((rows, dim), jnp.bfloat16)] * 2
    operands = [*q_slabs, *blocks, *(() if first else state)]
    return pl.pallas_call(
        functools.partial(attend_kernel, first, half, chunks),
        in_specs=[vmem] * len(operands),
        out_specs=[vmem] * len(out_shape),
        scratch_shapes=[
            pltpu.VMEM((2 * half, dim), jnp.bfloat16),
            pltpu.VMEM((keys, dim), jnp.bfloat16),
            pltpu.VMEM((keys, dim), jnp.bfloat16),
            pltpu.VMEM((8, keys), jnp.float32),
        ],
        out_shape=out_shape,
        cost_estimate=LIGHT,
        compiler_params=pltpu.CompilerParams(vmem_limit_bytes=ATTEND_VMEM),
    )(*operands)


def assemble_kernel(*refs):
    sources, mine, held, arrived = refs[:4], refs[4], refs[5], refs[6]
    x, y, z, core = position()
    odd = y % 2
    count, width = held.shape[:2]
    part = width // 2

    def fetch(j, action):
        wanted = (x + j) % count
        slot, arrival = held.at[j], arrived.at[j]

        @pl.when(z >= 2)
        def _():
            top = pl.multiple_of(wanted * width, width)
            action(pltpu.make_async_copy(mine.at[pl.ds(top, width)], slot, arrival))

        for n in range(2):

            @pl.when((z < 2) & ((wanted // 2 + z) % 2 == n))
            def _(n=n):
                for source, side in ((sources[n], core), (sources[2 + n], 1 - core)):
                    top = pl.multiple_of(side * part, part)
                    block = source.at[(wanted + odd) % 2]
                    action(pltpu.make_async_copy(block, slot.at[pl.ds(top, part)], arrival))

    for j in range(count):
        fetch(j, lambda copy: copy.start())
    for j in range(count):
        fetch(j, lambda copy: copy.wait())


def assemble(sources):
    count, (features, width) = 4, sources[4].shape
    shape = (count, features // count, width)
    return pl.pallas_call(
        assemble_kernel,
        in_specs=[pl.BlockSpec(memory_space=pl.ANY)] * 5,
        out_specs=pl.BlockSpec(memory_space=pltpu.VMEM),
        out_shape=jax.ShapeDtypeStruct(shape, jnp.bfloat16),
        scratch_shapes=[pltpu.SemaphoreType.DMA((count,))],
        cost_estimate=LIGHT,
        compiler_params=pltpu.CompilerParams(vmem_limit_bytes=SMALL_VMEM),
    )(*sources)


def project_kernel(distances, c0, c1, c2, c3, held, *refs):
    *out_refs, context = refs
    z = position()[2]
    dim = c0.shape[1]
    for d, ref in enumerate((c0, c1, c2, c3)):
        head = (z + 4 - d) % 4
        context[:, pl.ds(pl.multiple_of(head * dim, dim), dim)] = ref[...]
    parts = len(out_refs) // len(distances)
    for j, distance in enumerate(distances):
        mixed = lax.dot_general(
            context[...], held[distance], (((1,), (1,)), ((), ())), preferred_element_type=jnp.float32
        )
        for n, ref in enumerate(out_refs[j * parts : (j + 1) * parts]):
            size = ref.shape[0]
            ref[...] = mixed[n * size : (n + 1) * size].astype(ref.dtype)


def project(contexts, features, distances, dtypes):
    rows, dim = contexts[0].shape
    width = features.shape[1]
    outs = len(dtypes)
    parts = outs // len(distances)
    vmem = pl.BlockSpec(memory_space=pltpu.VMEM)
    return pl.pallas_call(
        functools.partial(project_kernel, distances),
        in_specs=[vmem] * 5,
        out_specs=[vmem] * outs,
        out_shape=[jax.ShapeDtypeStruct((rows // parts, width), dtype) for dtype in dtypes],
        scratch_shapes=[pltpu.VMEM((rows, 4 * dim), jnp.bfloat16)],
        cost_estimate=LIGHT,
        compiler_params=pltpu.CompilerParams(vmem_limit_bytes=SMALL_VMEM),
    )(*contexts, features)


def joined_kernel(up_ref, down_ref, upward, downward, up_out, down_out):
    up_out[...] = (up_ref[...] + upward[...].astype(jnp.float32)).astype(jnp.bfloat16)
    down_out[...] = (down_ref[...] + downward[...].astype(jnp.float32)).astype(jnp.bfloat16)


def joined(*operands):
    vmem = pl.BlockSpec(memory_space=pltpu.VMEM)
    return pl.pallas_call(
        joined_kernel,
        in_specs=[vmem] * 4,
        out_specs=[vmem] * 2,
        out_shape=[jax.ShapeDtypeStruct(operands[2].shape, jnp.bfloat16)] * 2,
        cost_estimate=LIGHT,
        compiler_params=pltpu.CompilerParams(vmem_limit_bytes=SMALL_VMEM),
    )(*operands)


def finish_kernel(residual, near_top, near_end, up_top, up_end, down_top, down_end, out_ref):
    half = up_top.shape[0]
    for top, near, one, other in ((0, near_top, up_top, down_top), (half, near_end, up_end, down_end)):
        rows = slice(top, top + half)
        found = residual[rows, :].astype(jnp.float32) + near[...]
        found = found + one[...].astype(jnp.float32) + other[...].astype(jnp.float32)
        out_ref[rows, :] = found.astype(jnp.bfloat16)


def finish(residual, *parts):
    vmem = pl.BlockSpec(memory_space=pltpu.VMEM)
    return pl.pallas_call(
        finish_kernel,
        in_specs=[vmem] * 7,
        out_specs=vmem,
        out_shape=jax.ShapeDtypeStruct(residual.shape, jnp.bfloat16),
        cost_estimate=LIGHT,
        compiler_params=pltpu.CompilerParams(vmem_limit_bytes=SMALL_VMEM),
    )(residual, *parts)


def position():
    segment, ctx, x = (lax.axis_index(axis) for axis in AXES)
    core, y, low = ctx % 2, (ctx // 2) % 4, ctx // 8
    return x, y, 2 * segment + low, core


def after(value, *others):
    return lax.optimization_barrier((value, *others))[0]


def local(targets, memory, pad_counts, norm_gains, proj_weights):
    segment, ctx, x = (lax.axis_index(axis) for axis in AXES)
    core, y, low = ctx % 2, (ctx // 2) % 4, ctx // 8
    z = 2 * segment + low
    model, width = proj_weights.shape[1], proj_weights.shape[3]
    dim = width * 4 // HEADS
    rows = targets.shape[0]
    half = model // 2
    chunks = 2
    down = lambda x, y, z, c: (x, y, 3 - z, c)
    encoder = lambda x, y, z, c: z < 2
    decoder = lambda x, y, z, c: z >= 2
    flip = lambda x, y, z, c: (x, y, 1 - z, c)
    is_encoder = segment == 0

    share = share_of(proj_weights, half // 8)
    p = moved(share, down, decoder)

    own, *to = section(after(pad_counts, share), memory, targets, norm_gains, proj_weights, dim)
    p = after(p, own)
    beside = moved(p, lambda x, y, z, c: (x, y ^ 1, z, c), encoder)
    r1, r3, r2 = along_z(to[0], 1), along_z(to[2], 3), along_z(to[1], 2)
    early = jnp.where(is_encoder, own, jnp.where(z == 2, r1, r3))
    late = jnp.where(z == 0, r3, jnp.where(z == 1, r1, r2))
    pair = jnp.stack([early, late])
    pair, p = lax.optimization_barrier((pair, p))

    y1, y3 = along_y(pair, 1), along_y(pair, 3)
    lower = jnp.stack([p, beside])
    upper = moved(lower, flip, encoder)
    (mine,) = second_half(after(proj_weights, pair), jnp.int32(2), half // 2, 2, 1)
    y1, y3, mine = lax.optimization_barrier((y1, y3, mine))

    far0, far1 = along_y(y1[0], 1), along_y(y3[1], 3)
    slabs = [own, r1, r2, r3]
    blocks = [pair, y1, y3]
    state = attend(slabs, blocks + [other_core(b) for b in blocks], chunks)
    far0, far1, *state = lax.optimization_barrier((far0, far1, *state))

    blocks = [far0[None], far1[None]]
    blocks = blocks + [other_core(b) for b in blocks]
    ca, cb = attend(slabs, blocks, chunks, state)
    lower_twin = other_core(after(lower, state[0]), encoder)
    upper_twin = other_core(after(upper, ca), encoder)
    contexts = [ca, along_z(cb, 1), along_z(ca, 2), along_z(cb, 3)]
    sources = [lower, upper, lower_twin, upper_twin, mine]
    out_width = model // 8
    residual = lax.dynamic_slice_in_dim(targets, (segment * 4 + x) * out_width, out_width, 1)
    features = assemble(sources)
    wide, narrow = jnp.float32, jnp.bfloat16
    wide, narrow = jnp.float32, jnp.bfloat16
    upward, downward = project(contexts, features, (2,), (narrow, narrow))
    contexts[0], upward, downward = lax.optimization_barrier((contexts[0], upward, downward))
    up_top, up_end, down_top, down_end, near_top, near_end = project(
        contexts, features, (1, 3, 0), (wide, narrow, narrow, wide, wide, wide)
    )
    up_end, down_top = along_x(up_end, 1), along_x(down_top, 3)
    up_top, down_end = joined(up_top, down_end, along_x(upward, 1), along_x(downward, 3))
    up_top, down_end = along_x(up_top, 1), along_x(down_end, 3)
    return finish(residual, near_top, near_end, up_top, up_end, down_top, down_end)


def solution(mesh):
    placed = (
        P("ctx", None),
        P("ctx", None),
        P("ctx"),
        P("segment", None),
        P("segment", None, None, "mp"),
    )
    return jax.shard_map(
        local, mesh=mesh, in_specs=placed, out_specs=P("ctx", ("segment", "mp")), check_vma=False
    )
```

```python
import functools

import jax
import jax.numpy as jnp
from jax import lax
from jax.experimental import pallas as pl
from jax.experimental.pallas import tpu as pltpu
from jax.sharding import PartitionSpec as P

HEADS = 16
AXES = ("segment", "ctx", "mp")
MARK_ROWS = 16
DEAD = -1e30
VMEM = 56 * 2**20
ATTEND_VMEM = 40 * 2**20
SMALL_VMEM = 24 * 2**20
LIGHT = pl.CostEstimate(flops=0, bytes_accessed=1024, transcendentals=0)


def device_of(x, y, z, core):
    return (z // 2) * 64 + (z % 2) * 32 + y * 8 + core * 4 + x


def place_of(i):
    return i % 4, (i // 8) % 4, (i // 64) * 2 + (i // 32) % 2, (i // 4) % 2


def moved(block, step, senders=lambda x, y, z, core: True):
    route = []
    for i in range(128):
        place = place_of(i)
        if senders(*place):
            x, y, z, core = step(*place)
            route.append((i, device_of(x % 4, y % 4, z % 4, core % 2)))
    return lax.ppermute(block, AXES, route)


def along_x(block, d):
    return moved(block, lambda x, y, z, c: (x + d, y, z, c))


def along_y(block, d, senders=lambda x, y, z, core: True):
    return moved(block, lambda x, y, z, c: (x, y + d, z, c), senders)


def along_z(block, d):
    return moved(block, lambda x, y, z, c: (x, y, z + d, c))


def other_core(block, senders=lambda x, y, z, core: True):
    return moved(block, lambda x, y, z, c: (x, y, z, c + 1), senders)


def norm_rows(hidden_rows, gain_row):
    widened = hidden_rows.astype(jnp.float32)
    inverse = lax.rsqrt(jnp.mean(widened * widened, axis=-1, keepdims=True) + 1e-06)
    return (widened * inverse * gain_row).astype(jnp.bfloat16)


def section_kernel(pad_ref, memory, targets, gain_ref, weights, *refs):
    *out_refs, normed, x_rows, total, blocks, arrival, block_arrival = refs
    steps, depth, _, width = blocks.shape
    rows = total.shape[0]
    half = rows // 2
    dim = out_refs[0].shape[1]
    z = position()[2]
    encoder = z < 2

    def block_copy(k):
        source = weights.at[0, pl.ds(pl.multiple_of(k * depth, depth), depth)]
        return pltpu.make_async_copy(source, blocks.at[k], block_arrival.at[k])

    def normalise(source, count):
        block = 128
        copies = [
            pltpu.make_async_copy(
                source.at[pl.ds(top, block)], x_rows.at[pl.ds(top, block)], arrival.at[top // block]
            )
            for top in range(0, count, block)
        ]
        for copy in copies:
            copy.start()
        for k in range(steps // 2):
            block_copy(k).start()
        for top in range(0, count, 64):
            if top % block == 0:
                copies[top // block].wait()
            part = norm_rows(x_rows[pl.ds(top, 64), :], gain_ref[...])
            for j in range(normed.shape[0]):
                normed[j, pl.ds(top, 64), :] = part[:, j * depth : (j + 1) * depth]

    @pl.when(encoder)
    def _():
        normalise(memory, half)

    @pl.when(jnp.logical_not(encoder))
    def _():
        normalise(targets, rows)

    for k in range(steps // 2, steps):
        block_copy(k).start()
    total[...] = jnp.zeros_like(total)

    @pl.loop(0, steps)
    def _(k):
        block_copy(k).wait()

        @pl.when(encoder)
        def _():
            both = blocks[k].reshape(depth, 2 * width)
            found = jnp.dot(normed[k, :half, :], both, preferred_element_type=jnp.float32)
            total[:half, :] += found[:, :width]
            total[half:, :] += found[:, width:]

        @pl.when(jnp.logical_not(encoder))
        def _():
            both = blocks[k].reshape(depth, 2 * width)
            total[...] += jnp.dot(normed[k], both[:, :width], preferred_element_type=jnp.float32)

    columns = lax.broadcasted_iota(jnp.int32, (MARK_ROWS, dim), 1)
    marks = jnp.where(columns < half - pad_ref[0], 0.0, DEAD).astype(jnp.bfloat16)
    for d, ref in enumerate(out_refs):
        head = (z + d) % 4
        ref[:rows, :] = total[:, pl.ds(pl.multiple_of(head * dim, dim), dim)].astype(jnp.bfloat16)
        ref[rows:, :] = marks


def section(pad_counts, memory, targets, gains, weights, dim):
    rows, model = targets.shape
    width = weights.shape[3]
    depth = 1024
    steps = model // depth
    slab = (rows + MARK_ROWS, dim)
    anywhere = pl.BlockSpec(memory_space=pl.ANY)
    vmem = pl.BlockSpec(memory_space=pltpu.VMEM)
    return pl.pallas_call(
        section_kernel,
        in_specs=[pl.BlockSpec(memory_space=pltpu.SMEM), anywhere, anywhere, vmem, anywhere],
        out_specs=[vmem] * 4,
        scratch_shapes=[
            pltpu.VMEM((steps, rows, depth), jnp.bfloat16),
            pltpu.VMEM((rows, model), jnp.bfloat16),
            pltpu.VMEM((rows, width), jnp.float32),
            pltpu.VMEM((steps, depth, 2, width), jnp.bfloat16),
            pltpu.SemaphoreType.DMA((rows // 128,)),
            pltpu.SemaphoreType.DMA((steps,)),
        ],
        out_shape=[jax.ShapeDtypeStruct(slab, jnp.bfloat16)] * 4,
        cost_estimate=LIGHT,
        compiler_params=pltpu.CompilerParams(vmem_limit_bytes=VMEM),
    )(pad_counts, memory, targets, gains, weights)


def second_half_kernel(start_ref, w_ref, *out_refs):
    depth, width = w_ref.shape[1], w_ref.shape[3]
    found = w_ref[0].reshape(depth, 2 * width)[:, width:]
    for j, ref in enumerate(out_refs):
        size = ref.shape[0]
        ref[...] = found[j * size : (j + 1) * size]


def second_half(weights, start, depth, steps, pieces):
    width = weights.shape[3]
    return pl.pallas_call(
        second_half_kernel,
        grid_spec=pltpu.PrefetchScalarGridSpec(
            num_scalar_prefetch=1,
            grid=(steps,),
            in_specs=[pl.BlockSpec((1, depth, 2, width), lambda k, start: (0, start[0] + k, 0, 0))],
            out_specs=[pl.BlockSpec((depth // pieces, width), lambda k, start: (k, 0))] * pieces,
        ),
        out_shape=[jax.ShapeDtypeStruct((steps * depth // pieces, width), jnp.bfloat16)] * pieces,
        cost_estimate=LIGHT,
        compiler_params=pltpu.CompilerParams(vmem_limit_bytes=VMEM),
    )(start.reshape(1), weights)


def share_kernel(w_ref, out_ref, held, arrived):
    x, y, z, core = position()
    size, width = out_ref.shape
    index = (2 * (1 - z % 2) + y % 2) * 2 + core
    top = pl.multiple_of(index * size, size)
    copy = pltpu.make_async_copy(w_ref.at[0, pl.ds(top, size)], held, arrived)
    copy.start()
    copy.wait()
    out_ref[...] = held[...].reshape(size, 2 * width)[:, width:]


def share_of(weights, size):
    width = weights.shape[3]
    return pl.pallas_call(
        share_kernel,
        in_specs=[pl.BlockSpec(memory_space=pl.ANY)],
        out_specs=pl.BlockSpec(memory_space=pltpu.VMEM),
        out_shape=jax.ShapeDtypeStruct((size, width), jnp.bfloat16),
        scratch_shapes=[pltpu.VMEM((size, 2, width), jnp.bfloat16), pltpu.SemaphoreType.DMA],
        cost_estimate=LIGHT,
        compiler_params=pltpu.CompilerParams(vmem_limit_bytes=VMEM),
    )(weights)


def attend_kernel(first, half, chunks, *refs):
    if first:
        *slabs, acc_ref, peak_ref, total_ref, queries, keys, values, marks = refs
    else:
        *slabs, acc_ref, peak_ref, total_ref, out_a, out_b, queries, keys, values, marks = refs
    q_slabs, blocks = slabs[:4], slabs[4:]
    size = (blocks[0].shape[1] - MARK_ROWS) // 2
    z = position()[2]
    pieces = [ref.at[n] for ref in blocks for n in range(ref.shape[0])]
    for j, ref in enumerate(pieces):
        keys[j * size : (j + 1) * size, :] = ref[:size, :]
        values[j * size : (j + 1) * size, :] = ref[size : 2 * size, :]
        marks[:, j * size : (j + 1) * size] = ref[2 * size : 2 * size + MARK_ROWS, :].astype(jnp.float32)

    def run(at):
        base = at * 2 * half

        def take(index, when, top):
            @pl.when(when)
            def _():
                queries[pl.ds(top, half), :] = q_slabs[index][at * half : (at + 1) * half, :]

        take(2, z < 2, 0)
        take(0, z >= 2, 0)
        inner = (z == 1) | (z == 2)
        take(3, inner, half)
        take(1, jnp.logical_not(inner), half)

        part = 256
        for top in range(0, 2 * half, part):
            scores = lax.dot_general(
                queries[top : top + part, :],
                keys[...],
                (((1,), (1,)), ((), ())),
                preferred_element_type=jnp.float32,
            )
            scores = scores + marks[0:1, :]
            peak = jnp.max(scores, axis=1, keepdims=True)
            mine = slice(base + top, base + top + part)
            if not first:
                before = peak_ref[mine, :1]
                peak = jnp.maximum(peak, before)
                scale = jnp.exp(before - peak)
            soft = jnp.exp(scores - peak)
            total = jnp.sum(soft, axis=1, keepdims=True)
            mixed = jnp.dot(
                soft.astype(jnp.bfloat16), values[...], preferred_element_type=jnp.float32
            )
            if first:
                acc_ref[mine, :] = mixed
                peak_ref[mine, :] = jnp.broadcast_to(peak, (part, 128))
                total_ref[mine, :] = jnp.broadcast_to(total, (part, 128))
            else:
                mixed = mixed + scale * acc_ref[mine, :]
                total = total + scale * total_ref[mine, :1]
                found = (mixed / total).astype(jnp.bfloat16)
                if top < half:
                    out_a[at * half + top : at * half + top + part, :] = found
                else:
                    out_b[at * half + top - half : at * half + top - half + part, :] = found

    for at in range(chunks):
        run(at)


def attend(q_slabs, blocks, chunks, state=None):
    rows, dim = q_slabs[0].shape[0] - MARK_ROWS, q_slabs[0].shape[1]
    half = rows // chunks
    first = state is None
    keys = sum(b.shape[0] for b in blocks) * (blocks[0].shape[1] - MARK_ROWS) // 2
    vmem = pl.BlockSpec(memory_space=pltpu.VMEM)
    if first:
        out_shape = [jax.ShapeDtypeStruct((2 * rows, last), jnp.float32) for last in (dim, 128, 128)]
    else:
        out_shape = [jax.ShapeDtypeStruct((rows, dim), jnp.bfloat16)] * 2
    operands = [*q_slabs, *blocks, *(() if first else state)]
    return pl.pallas_call(
        functools.partial(attend_kernel, first, half, chunks),
        in_specs=[vmem] * len(operands),
        out_specs=[vmem] * len(out_shape),
        scratch_shapes=[
            pltpu.VMEM((2 * half, dim), jnp.bfloat16),
            pltpu.VMEM((keys, dim), jnp.bfloat16),
            pltpu.VMEM((keys, dim), jnp.bfloat16),
            pltpu.VMEM((MARK_ROWS, keys), jnp.float32),
        ],
        out_shape=out_shape,
        cost_estimate=LIGHT,
        compiler_params=pltpu.CompilerParams(vmem_limit_bytes=ATTEND_VMEM),
    )(*operands)


def assemble_kernel(*refs):
    sources, mine, held, arrived = refs[:4], refs[4], refs[5], refs[6]
    x, y, z, core = position()
    odd = y % 2
    count, width = held.shape[:2]
    part = width // 2

    def fetch(j, action):
        wanted = (x + j) % count
        slot, arrival = held.at[j], arrived.at[j]

        @pl.when(z >= 2)
        def _():
            top = pl.multiple_of(wanted * width, width)
            action(pltpu.make_async_copy(mine.at[pl.ds(top, width)], slot, arrival))

        for n in range(2):

            @pl.when((z < 2) & ((wanted // 2 + z) % 2 == n))
            def _(n=n):
                for source, side in ((sources[n], core), (sources[2 + n], 1 - core)):
                    top = pl.multiple_of(side * part, part)
                    block = source.at[(wanted + odd) % 2]
                    action(pltpu.make_async_copy(block, slot.at[pl.ds(top, part)], arrival))

    for j in range(count):
        fetch(j, lambda copy: copy.start())
    for j in range(count):
        fetch(j, lambda copy: copy.wait())


def assemble(sources):
    count, (features, width) = 4, sources[4].shape
    shape = (count, features // count, width)
    return pl.pallas_call(
        assemble_kernel,
        in_specs=[pl.BlockSpec(memory_space=pl.ANY)] * 5,
        out_specs=pl.BlockSpec(memory_space=pltpu.VMEM),
        out_shape=jax.ShapeDtypeStruct(shape, jnp.bfloat16),
        scratch_shapes=[pltpu.SemaphoreType.DMA((count,))],
        cost_estimate=LIGHT,
        compiler_params=pltpu.CompilerParams(vmem_limit_bytes=SMALL_VMEM),
    )(*sources)


def project_kernel(distances, c0, c1, c2, c3, held, *refs):
    *out_refs, context = refs
    z = position()[2]
    dim = c0.shape[1]
    for d, ref in enumerate((c0, c1, c2, c3)):
        head = (z + 4 - d) % 4
        context[:, pl.ds(pl.multiple_of(head * dim, dim), dim)] = ref[...]
    parts = len(out_refs) // len(distances)
    for j, distance in enumerate(distances):
        mixed = lax.dot_general(
            context[...], held[distance], (((1,), (1,)), ((), ())), preferred_element_type=jnp.float32
        )
        for n, ref in enumerate(out_refs[j * parts : (j + 1) * parts]):
            size = ref.shape[0]
            ref[...] = mixed[n * size : (n + 1) * size].astype(ref.dtype)


def project(contexts, features, distances, dtypes):
    rows, dim = contexts[0].shape
    width = features.shape[1]
    outs = len(dtypes)
    parts = outs // len(distances)
    vmem = pl.BlockSpec(memory_space=pltpu.VMEM)
    return pl.pallas_call(
        functools.partial(project_kernel, distances),
        in_specs=[vmem] * 5,
        out_specs=[vmem] * outs,
        out_shape=[jax.ShapeDtypeStruct((rows // parts, width), dtype) for dtype in dtypes],
        scratch_shapes=[pltpu.VMEM((rows, 4 * dim), jnp.bfloat16)],
        cost_estimate=LIGHT,
        compiler_params=pltpu.CompilerParams(vmem_limit_bytes=SMALL_VMEM),
    )(*contexts, features)


def joined_kernel(up_ref, down_ref, upward, downward, up_out, down_out):
    up_out[...] = (up_ref[...] + upward[...].astype(jnp.float32)).astype(jnp.bfloat16)
    down_out[...] = (down_ref[...] + downward[...].astype(jnp.float32)).astype(jnp.bfloat16)


def joined(*operands):
    vmem = pl.BlockSpec(memory_space=pltpu.VMEM)
    return pl.pallas_call(
        joined_kernel,
        in_specs=[vmem] * 4,
        out_specs=[vmem] * 2,
        out_shape=[jax.ShapeDtypeStruct(operands[2].shape, jnp.bfloat16)] * 2,
        cost_estimate=LIGHT,
        compiler_params=pltpu.CompilerParams(vmem_limit_bytes=SMALL_VMEM),
    )(*operands)


def finish_kernel(residual, near_top, near_end, up_top, up_end, down_top, down_end, out_ref):
    half = up_top.shape[0]
    for top, near, one, other in ((0, near_top, up_top, down_top), (half, near_end, up_end, down_end)):
        rows = slice(top, top + half)
        found = residual[rows, :].astype(jnp.float32) + near[...]
        found = found + one[...].astype(jnp.float32) + other[...].astype(jnp.float32)
        out_ref[rows, :] = found.astype(jnp.bfloat16)


def finish(residual, *parts):
    vmem = pl.BlockSpec(memory_space=pltpu.VMEM)
    return pl.pallas_call(
        finish_kernel,
        in_specs=[vmem] * 7,
        out_specs=vmem,
        out_shape=jax.ShapeDtypeStruct(residual.shape, jnp.bfloat16),
        cost_estimate=LIGHT,
        compiler_params=pltpu.CompilerParams(vmem_limit_bytes=SMALL_VMEM),
    )(residual, *parts)


def position():
    segment, ctx, x = (lax.axis_index(axis) for axis in AXES)
    core, y, low = ctx % 2, (ctx // 2) % 4, ctx // 8
    return x, y, 2 * segment + low, core


def after(value, *others):
    return lax.optimization_barrier((value, *others))[0]


def local(targets, memory, pad_counts, norm_gains, proj_weights):
    segment, ctx, x = (lax.axis_index(axis) for axis in AXES)
    core, y, low = ctx % 2, (ctx // 2) % 4, ctx // 8
    z = 2 * segment + low
    model, width = proj_weights.shape[1], proj_weights.shape[3]
    dim = width * 4 // HEADS
    rows = targets.shape[0]
    half = model // 2
    chunks = 2
    down = lambda x, y, z, c: (x, y, 3 - z, c)
    encoder = lambda x, y, z, c: z < 2
    decoder = lambda x, y, z, c: z >= 2
    flip = lambda x, y, z, c: (x, y, 1 - z, c)
    is_encoder = segment == 0

    share = share_of(proj_weights, half // 8)
    p = moved(share, down, decoder)

    own, *to = section(after(pad_counts, share), memory, targets, norm_gains, proj_weights, dim)
    p = after(p, own)
    beside = moved(p, lambda x, y, z, c: (x, y ^ 1, z, c), encoder)
    r1, r3, r2 = along_z(to[0], 1), along_z(to[2], 3), along_z(to[1], 2)
    early = jnp.where(is_encoder, own, jnp.where(z == 2, r1, r3))
    late = jnp.where(z == 0, r3, jnp.where(z == 1, r1, r2))
    pair = jnp.stack([early, late])
    pair, p = lax.optimization_barrier((pair, p))

    y1, y3 = along_y(pair, 1), along_y(pair, 3)
    lower = jnp.stack([p, beside])
    upper = moved(lower, flip, encoder)
    (mine,) = second_half(after(proj_weights, pair), jnp.int32(2), half // 2, 2, 1)
    y1, y3, mine = lax.optimization_barrier((y1, y3, mine))

    far0, far1 = along_y(y1[0], 1), along_y(y3[1], 3)
    slabs = [own, r1, r2, r3]
    blocks = [pair, y1, y3]
    state = attend(slabs, blocks + [other_core(b) for b in blocks], chunks)
    far0, far1, *state = lax.optimization_barrier((far0, far1, *state))

    blocks = [far0[None], far1[None]]
    blocks = blocks + [other_core(b) for b in blocks]
    ca, cb = attend(slabs, blocks, chunks, state)
    lower_twin = other_core(after(lower, state[0]), encoder)
    upper_twin = other_core(after(upper, ca), encoder)
    contexts = [ca, along_z(cb, 1), along_z(ca, 2), along_z(cb, 3)]
    sources = [lower, upper, lower_twin, upper_twin, mine]
    out_width = model // 8
    residual = lax.dynamic_slice_in_dim(targets, (segment * 4 + x) * out_width, out_width, 1)
    features = assemble(sources)
    wide, narrow = jnp.float32, jnp.bfloat16
    wide, narrow = jnp.float32, jnp.bfloat16
    upward, downward = project(contexts, features, (2,), (narrow, narrow))
    contexts[0], upward, downward = lax.optimization_barrier((contexts[0], upward, downward))
    up_top, up_end, down_top, down_end, near_top, near_end = project(
        contexts, features, (1, 3, 0), (wide, narrow, narrow, wide, wide, wide)
    )
    up_end, down_top = along_x(up_end, 1), along_x(down_top, 3)
    up_top, down_end = joined(up_top, down_end, along_x(upward, 1), along_x(downward, 3))
    up_top, down_end = along_x(up_top, 1), along_x(down_end, 3)
    return finish(residual, near_top, near_end, up_top, up_end, down_top, down_end)


def solution(mesh):
    placed = (
        P("ctx", None),
        P("ctx", None),
        P("ctx"),
        P("segment", None),
        P("segment", None, None, "mp"),
    )
    return jax.shard_map(
        local, mesh=mesh, in_specs=placed, out_specs=P("ctx", ("segment", "mp")), check_vma=False
    )
```
